32 devices in a mesh: scene: 1, panel: 16 (over z, y, x), aper: 2 (over core).
Axes of the slice: x: 2, y: 2, z: 4, core: 2. Of those that a mesh axis runs over, the one named last changes fastest.
Arguments:
- subimages: bfloat16 [4, 2, 512, 4096], P(('scene', 'aper'), None, 'panel'), may hold values from -6 to 6
- rng_taps: int32 [2, 3, 512], P('aper'), may hold values from 0 to 240
- rng_blocks: int32 [2, 3, 4], P('aper'), may hold values from 0 to 2, as said below
- rng_weights: bfloat16 [2, 3, 2, 16, 512], P('aper'), may hold values from -0.75 to 0.75
- ang_taps: int32 [2, 32768], P('aper'), may hold values from 0 to 240
- ang_blocks: int32 [2, 256], P('aper'), may hold values from 0 to 62, as said below
- ang_weights: bfloat16 [2, 2, 16, 32768], P('aper'), may hold values from -0.75 to 0.75
- owners: int32 [16384], replicated, may hold values from 0 to 63
Outputs:
- image: bfloat16 [2, 512, 16384], P(None, ('scene', 'aper'), 'panel')
- gradients: float32 [2, 64], P(('scene', 'aper'), 'panel')
The draws below stay inside these ranges and needn't reach their ends.
Inputs may be any that keep to these rules, and one draw needn't show every extreme that they name: `ang_blocks`: numbering the output angle blocks of one slot from the start of its columns as j, block j reads input blocks starting at j // 2 - 1 or j // 2, kept within 0 to the slot's input blocks minus 2 (input blocks: 32 for slots 0 and 1, 64 for slot 2). `rng_blocks`: output range block j reads input blocks starting at j - 1 or j, kept within 0 to 2.
All inputs are finite; a program needn't handle non-finite values.
Results may differ from the reference program's by a relative error of at most 0.0071.
Values may be sent and summed in bfloat16 or wider, within the bound.
No kernel may reach another device: no remote copies, remote signals or barrier semaphores. Data moves between devices by JAX's collectives and lax.ppermute only.
A program may use at most 192 MiB of HBM per device.

```python
import jax
import jax.numpy as jnp
from jax import lax

ANG_C = 4096
TILE = 128
TAPS = 16
RANGE = 512
ANG_P = 8192
ANG_F = 16384
ANG_ALL = 32768
SUBAPS = 4
GROUPS = 64
N_APER = 2


def draw_ang_blocks(key, part):
    first = ANG_P // TILE
    second = ANG_F // TILE
    local = jnp.concatenate([jnp.arange(first, dtype=jnp.int32), jnp.arange(first, dtype=jnp.int32), jnp.arange(second, dtype=jnp.int32)])
    limit = jnp.concatenate([jnp.full((first,), ANG_C // TILE - 2, jnp.int32), jnp.full((first,), ANG_C // TILE - 2, jnp.int32), jnp.full((second,), ANG_P // TILE - 2, jnp.int32)])
    coin = jax.random.randint(key, (N_APER, 2 * first + second), 0, 2, dtype=jnp.int32)
    return jnp.clip(local[None, :] // 2 - coin, 0, limit[None, :]).astype(jnp.int32)


def draw_rng_blocks(key, part):
    count = RANGE // TILE
    local = jnp.arange(count, dtype=jnp.int32)
    coin = jax.random.randint(jax.random.fold_in(key, 7), (N_APER, 3, count), 0, 2, dtype=jnp.int32)
    return jnp.clip(local[None, None, :] - coin, 0, count - 2).astype(jnp.int32)


def with_ends(array, rng, least, largest):
    extent = array.shape
    index_at = [jax.random.randint(jax.random.fold_in(rng, axis), (), 0, extent[axis]) for axis in range(len(extent))]
    array = array.at[tuple(index_at)].set(least)
    longest = extent.index(max(extent))
    index_at[longest] = (index_at[longest] + 1) % extent[longest]
    return array.at[tuple(index_at)].set(largest)


def block_levels(rng, shape, split, smallest, high):
    def one(axis_at, blocks):
        heights = jax.random.uniform(jax.random.fold_in(jax.random.fold_in(rng, 6), axis_at), (blocks,), jnp.float32, smallest / len(split), high / len(split))
        return jnp.repeat(jnp.exp(heights), shape[axis_at] // blocks).reshape((-1,) + (1,) * (len(shape) - axis_at - 1))

    factor_of = one(*split[0])
    for cut in split[1:]:
        factor_of = factor_of * one(*cut)
    return factor_of


def centred(key, extent, scale, most, pieces=(), held_as=jnp.bfloat16):
    entries = scale * jax.random.normal(key, extent, jnp.float32)
    if pieces:
        entries = entries * block_levels(key, extent, pieces, -0.22, 0.18)
    return jnp.clip(entries, -most, most).astype(held_as)


def setup_inputs(seed: int = 0, part: int = 0) -> dict:
    streams_of = jax.random.split(jax.random.key(seed), 9)
    own_keys = jax.random.split(jax.random.fold_in(streams_of[8], part), 9)
    subimages = centred(own_keys[0], (SUBAPS, 2, RANGE, ANG_C), 1.0, 6.0, ((0, 2), (2, 16)))
    rng_taps = with_ends(jax.random.randint(streams_of[1], (N_APER, 3, RANGE), 0, 2 * TILE - TAPS + 1), jax.random.fold_in(streams_of[1], 1), 0, 2 * TILE - TAPS).astype(jnp.int32)
    rng_blocks = draw_rng_blocks(jax.random.fold_in(streams_of[8], 71), part)
    rng_weights = centred(streams_of[3], (N_APER, 3, 2, TAPS, RANGE), (4 * TAPS) ** -0.5, 0.75, ((0, 2),))
    ang_taps = with_ends(jax.random.randint(streams_of[4], (N_APER, ANG_ALL), 0, 2 * TILE - TAPS + 1), jax.random.fold_in(streams_of[4], 1), 0, 2 * TILE - TAPS).astype(jnp.int32)
    ang_blocks = draw_ang_blocks(jax.random.fold_in(streams_of[8], 71), part)
    ang_weights = centred(streams_of[6], (N_APER, 2, TAPS, ANG_ALL), (4 * TAPS) ** -0.5, 0.75, ((0, 2),))
    owners = with_ends(jax.random.randint(streams_of[7], (ANG_F,), 0, GROUPS), jax.random.fold_in(streams_of[7], 1), 0, GROUPS - 1).astype(jnp.int32)
    return dict(subimages=subimages, rng_taps=rng_taps, rng_blocks=rng_blocks, rng_weights=rng_weights, ang_taps=ang_taps, ang_blocks=ang_blocks, ang_weights=ang_weights, owners=owners)


def build_tiles(base, weights):
    span = jnp.arange(2 * TILE, dtype=jnp.int32)
    offset = span[None, :, None] - base[:, None, :]
    tiles = jnp.zeros((2,) + offset.shape, weights.dtype)
    for tap in range(TAPS):
        chosen = weights[:, tap][:, :, None, :]
        tiles = tiles + jnp.where((offset == tap)[None], chosen, jnp.zeros((), weights.dtype))
    return tiles


def angle_pass(child, starts, base, weights):
    rows = child.shape[1]
    count = starts.shape[0]
    blocks = child.reshape(2, rows, child.shape[2] // TILE, TILE)
    spans = jnp.concatenate([jnp.take(blocks, starts, axis=2), jnp.take(blocks, starts + 1, axis=2)], axis=3)
    tiles = build_tiles(base.reshape(count, TILE), weights.reshape(2, TAPS, count, TILE))

    def product(left, right):
        return jnp.einsum("rnk,nka->rna", left.astype(jnp.float32), right.astype(jnp.float32), precision=lax.Precision.HIGHEST)

    real = product(spans[0], tiles[0]) - product(spans[1], tiles[1])
    imag = product(spans[0], tiles[1]) + product(spans[1], tiles[0])
    return jnp.stack([real, imag]).reshape(2, rows, count * TILE)


def range_pass(child, starts, base, weights):
    cols = child.shape[2]
    count = starts.shape[0]
    blocks = child.reshape(2, child.shape[1] // TILE, TILE, cols)
    spans = jnp.concatenate([jnp.take(blocks, starts, axis=1), jnp.take(blocks, starts + 1, axis=1)], axis=2)
    tiles = build_tiles(base.reshape(count, TILE), weights.reshape(2, TAPS, count, TILE))

    def product(left, right):
        return jnp.einsum("nkr,nkc->nrc", left.astype(jnp.float32), right.astype(jnp.float32), precision=lax.Precision.HIGHEST)

    real = product(tiles[0], spans[0]) - product(tiles[1], spans[1])
    imag = product(tiles[0], spans[1]) + product(tiles[1], spans[0])
    return jnp.stack([real, imag]).reshape(2, count * TILE, cols)


def reference(subimages, rng_taps, rng_blocks, rng_weights, ang_taps, ang_blocks, ang_weights, owners):
    contributions = []
    for side in range(2):
        total = None
        for member in range(2):
            ranged = range_pass(subimages[2 * side + member], rng_blocks[side, member], rng_taps[side, member], rng_weights[side, member]).astype(jnp.bfloat16)
            start = member * ANG_P
            term = angle_pass(ranged, ang_blocks[side, start // TILE:(start + ANG_P) // TILE], ang_taps[side, start:start + ANG_P], ang_weights[side, :, :, start:start + ANG_P])
            total = term if total is None else total + term
        merged = total.astype(jnp.bfloat16)
        second = range_pass(merged, rng_blocks[side, 2], rng_taps[side, 2], rng_weights[side, 2]).astype(jnp.bfloat16)
        start = 2 * ANG_P
        contributions.append(angle_pass(second, ang_blocks[side, start // TILE:(start + ANG_F) // TILE], ang_taps[side, start:start + ANG_F], ang_weights[side, :, :, start:start + ANG_F]).astype(jnp.bfloat16))
    focused = contributions[0].astype(jnp.float32) + contributions[1].astype(jnp.float32)
    place = jnp.arange(RANGE, dtype=jnp.int32).astype(jnp.float32)
    weight = 1.0 + 2.0 * place / (RANGE - 1)
    power = focused[0] * focused[0] + focused[1] * focused[1]
    marks = owners[:, None] == jnp.arange(GROUPS, dtype=jnp.int32)[None, :]
    gradients = []
    for side in range(2):
        own = contributions[side].astype(jnp.float32)
        inphase = focused[0] * own[0] + focused[1] * own[1]
        slope = jnp.sum(weight[:, None] * power * inphase, axis=0) / RANGE
        gradients.append(jnp.sum(jnp.where(marks, slope[:, None], jnp.zeros((), slope.dtype)), axis=0))
    return focused.astype(jnp.bfloat16), jnp.stack(gradients)
```

```python
import functools

import jax
import jax.numpy as jnp
from jax import lax
from jax.experimental import pallas as pl
from jax.experimental.pallas import tpu as pltpu
from jax.sharding import PartitionSpec as P

TILE = 128
PAIR = 2 * TILE
TAPS = 16
GRP_DEV = 4
F32 = jnp.float32
BF16 = jnp.bfloat16
VMEM_BYTES = 44 * 1024 * 1024


def aligned(value, step):
    return pl.multiple_of(value * step, step)


def params():
    return pltpu.CompilerParams(vmem_limit_bytes=VMEM_BYTES)


class Plan:
    def __init__(self, panels, rows, angles):
        self.panels = panels
        self.rows = rows
        self.total_rows = rows * panels
        self.in_blocks = angles // TILE
        self.own = self.in_blocks // panels
        self.cells = TILE // rows
        self.planes = panels // self.cells
        self.range_blocks = self.total_rows // TILE
        self.plane_window = min(self.cells * self.own + 4, self.in_blocks)
        self.panel_window = self.own + 4
        self.merged_window = 2 * self.own + 2
        self.out_blocks = 4 * self.own

    def plane_start(self, plane):
        return jnp.clip(
            self.cells * self.own * plane - 2, 0, self.in_blocks - self.plane_window
        )

    def panel_start(self, panel):
        return jnp.clip(self.own * panel - 2, 0, self.in_blocks - self.panel_window)

    def merged_start(self, panel):
        return jnp.clip(
            2 * self.own * panel - 1, 0, 2 * self.in_blocks - self.merged_window
        )


SMEM = pl.BlockSpec(memory_space=pltpu.SMEM)
VMEM = pl.BlockSpec(memory_space=pltpu.VMEM)


def pack_planes(plan, where, subimages):
    members = subimages.shape[0]

    def body(where_ref, x_ref, *outs):
        plane = where_ref[0] // plan.cells
        for step in range(plan.planes):
            start = plan.plane_start(lax.rem(plane + step, plan.planes))
            for member in range(members):
                out = outs[member * plan.planes + step]
                for block in range(plan.plane_window):
                    column = aligned(start + block, TILE)
                    for part in range(2):
                        at = block * PAIR + part * TILE
                        out[:, at : at + TILE] = x_ref[
                            member, part, :, pl.ds(column, TILE)
                        ]

    shape = jax.ShapeDtypeStruct((plan.rows, plan.plane_window * PAIR), BF16)
    outs = pl.pallas_call(
        body,
        out_shape=[shape] * (members * plan.planes),
        in_specs=[SMEM, VMEM],
        out_specs=[VMEM] * (members * plan.planes),
        compiler_params=params(),
        name="pack_planes",
    )(where, subimages)
    return [
        outs[member * plan.planes : (member + 1) * plan.planes]
        for member in range(members)
    ]


def pack_panels(plan, where, received):
    def body(where_ref, *refs):
        ins = refs[: plan.planes]
        outs = refs[plan.planes :]
        panel = where_ref[0]
        plane = panel // plan.cells
        cell = lax.rem(panel, plan.cells)
        base = plan.plane_start(plane)
        for flip in range(plan.cells):
            other = plane * plan.cells + (cell ^ flip)
            offset = plan.panel_start(other) - base
            for step in range(plan.planes):
                source = lax.rem(plane + plan.planes - step, plan.planes)
                outs[flip][source] = ins[step][
                    :, pl.ds(aligned(offset, PAIR), plan.panel_window * PAIR)
                ]

    shape = jax.ShapeDtypeStruct(
        (plan.planes, plan.rows, plan.panel_window * PAIR), BF16
    )
    return pl.pallas_call(
        body,
        out_shape=[shape] * plan.cells,
        in_specs=[SMEM] + [VMEM] * plan.planes,
        out_specs=[VMEM] * plan.cells,
        compiler_params=params(),
        name="pack_panels",
    )(where, *received)


def spread_taps(base, weights):
    low = base & (TAPS - 1)
    high = base >> 4
    wide = jnp.concatenate([weights, jnp.zeros_like(weights)], axis=0)
    for bit in range(4):
        moved = pltpu.roll(wide, 1 << bit, axis=0)
        wide = jnp.where(((low >> bit) & 1) == 1, moved, wide)
    zero = jnp.zeros_like(weights)
    pieces = []
    for place in range(PAIR // TAPS):
        below = jnp.where(high == place - 1, wide[TAPS:], zero)
        pieces.append(jnp.where(high == place, wide[:TAPS], below))
    return pieces


def build_angle(blocks, taps, weights):
    count = blocks.shape[0]

    def body(blocks_ref, taps_ref, weights_ref, out_ref):
        base = taps_ref[...]
        real = spread_taps(base, weights_ref[0].astype(F32))
        imag = spread_taps(base, weights_ref[1].astype(F32))
        half = TILE // TAPS
        for place in range(PAIR // TAPS):
            row = (place // half) * PAIR + (place % half) * TAPS
            re = real[place].astype(BF16)
            im = imag[place].astype(BF16)
            neg = (-imag[place]).astype(BF16)
            out_ref[0, row : row + TAPS, :TILE] = re
            out_ref[0, row : row + TAPS, TILE:] = im
            out_ref[0, TILE + row : TILE + row + TAPS, :TILE] = neg
            out_ref[0, TILE + row : TILE + row + TAPS, TILE:] = re

    return pl.pallas_call(
        body,
        out_shape=jax.ShapeDtypeStruct((count, 2 * PAIR, PAIR), BF16),
        grid_spec=pltpu.PrefetchScalarGridSpec(
            num_scalar_prefetch=1,
            grid=(count,),
            in_specs=[
                pl.BlockSpec((1, TILE), lambda i, t: (0, t[i])),
                pl.BlockSpec((2, TAPS, TILE), lambda i, t: (0, 0, t[i])),
            ],
            out_specs=pl.BlockSpec((1, 2 * PAIR, PAIR), lambda i, t: (i, 0, 0)),
        ),
        compiler_params=params(),
        name="build_angle",
    )(blocks, taps, weights)


def build_range(plan, taps, weights):
    slots = taps.shape[0]

    def body(taps_ref, weights_ref, out_ref):
        base = taps_ref[0]
        for part in range(2):
            pieces = spread_taps(base, weights_ref[0, part].astype(F32))
            matrix = jnp.concatenate(pieces, axis=0)
            out_ref[0, 0, part * TILE : (part + 1) * TILE, :] = matrix.T.astype(BF16)

    return pl.pallas_call(
        body,
        out_shape=jax.ShapeDtypeStruct((slots, plan.range_blocks, PAIR, PAIR), BF16),
        grid=(slots, plan.range_blocks),
        in_specs=[
            pl.BlockSpec((1, 1, TILE), lambda s, j: (s, 0, j)),
            pl.BlockSpec((1, 2, TAPS, TILE), lambda s, j: (s, 0, 0, j)),
        ],
        out_specs=pl.BlockSpec((1, 1, PAIR, PAIR), lambda s, j: (s, j, 0, 0)),
        compiler_params=params(),
        name="build_range",
    )(taps.reshape(slots, 1, -1), weights)


def range_step(plan, starts, matrices, source, target, blocks):
    for j in range(plan.range_blocks):
        rows = pl.ds(aligned(starts(j), TILE), PAIR)
        for block in range(blocks):
            at = block * PAIR
            res = jnp.dot(
                matrices[0, j], source[rows, at : at + PAIR], preferred_element_type=F32
            )
            real = res[:TILE, :TILE] - res[TILE:, TILE:]
            imag = res[:TILE, TILE:] + res[TILE:, :TILE]
            out = slice(j * TILE, (j + 1) * TILE)
            target[out, at : at + TILE] = real.astype(BF16)
            target[out, at + TILE : at + PAIR] = imag.astype(BF16)


def gather_rows(plan, panel, parts, target):
    cell = lax.rem(panel, plan.cells)
    for flip in range(plan.cells):
        source = cell ^ flip
        for plane in range(plan.planes):
            row = aligned(plane * plan.cells + source, plan.rows)
            target[pl.ds(row, plan.rows), :] = parts[flip][plane]


def first_member(plan, where, parts, rng_blocks, ang_blocks, rng_mats, ang_mats):
    def body(where_ref, rb_ref, ab_ref, *refs):
        ins = refs[: plan.cells]
        rm_ref, am_ref, out_ref, x_ref, z_ref = refs[plan.cells :]
        panel = where_ref[0]
        gather_rows(plan, panel, ins, x_ref)
        range_step(plan, lambda j: rb_ref[0, j], rm_ref, x_ref, z_ref, plan.panel_window)
        first = plan.merged_start(panel)
        base = plan.panel_start(panel)
        for j in range(plan.merged_window):
            start = ab_ref[0, first + j] - base
            out_ref[:, j * PAIR : (j + 1) * PAIR] = jnp.dot(
                z_ref[:, pl.ds(aligned(start, PAIR), 2 * PAIR)],
                am_ref[j],
                preferred_element_type=F32,
            )

    width = plan.panel_window * PAIR
    mwidth = plan.merged_window * PAIR
    return pl.pallas_call(
        body,
        out_shape=jax.ShapeDtypeStruct((plan.total_rows, mwidth), F32),
        grid=(1,),
        in_specs=[SMEM, SMEM, SMEM]
        + [VMEM] * plan.cells
        + [
            pl.BlockSpec((1, plan.range_blocks, PAIR, PAIR), lambda i: (0, 0, 0, 0)),
            pl.BlockSpec((plan.merged_window, 2 * PAIR, PAIR), lambda i: (0, 0, 0)),
        ],
        out_specs=VMEM,
        scratch_shapes=[pltpu.VMEM((plan.total_rows, width), BF16)] * 2,
        compiler_params=params(),
        name="first_member",
    )(where, rng_blocks, ang_blocks, *parts, rng_mats, ang_mats)


def second_member(
    plan, where, parts, partial, rng_blocks, ang_blocks, rng_mats, ang_mats, last_mats
):
    half = plan.total_rows // 2

    def body(where_ref, rb_ref, ab_ref, *refs):
        ins = refs[: plan.cells]
        (m_ref, rm_ref, r2_ref, am_ref, a2_ref, own_ref, send_ref) = refs[
            plan.cells : plan.cells + 7
        ]
        x_ref, z_ref, y_ref, s_ref = refs[plan.cells + 7 :]
        panel = where_ref[0]
        side = where_ref[1]
        gather_rows(plan, panel, ins, x_ref)
        range_step(plan, lambda j: rb_ref[1, j], rm_ref, x_ref, z_ref, plan.panel_window)
        first = plan.merged_start(panel)
        base = plan.panel_start(panel)
        for j in range(plan.merged_window):
            start = ab_ref[0, 2 * plan.in_blocks + first + j] - base
            term = jnp.dot(
                z_ref[:, pl.ds(aligned(start, PAIR), 2 * PAIR)],
                am_ref[j],
                preferred_element_type=F32,
            )
            at = slice(j * PAIR, (j + 1) * PAIR)
            y_ref[:, at] = (m_ref[:, at] + term).astype(BF16)
        range_step(plan, lambda j: rb_ref[2, j], r2_ref, y_ref, s_ref, plan.merged_window)
        for j in range(plan.out_blocks):
            place = 4 * plan.in_blocks + panel * plan.out_blocks + j
            columns = pl.ds(aligned(ab_ref[0, place] - first, PAIR), 2 * PAIR)
            for which, ref in ((1 - side, send_ref), (side, own_ref)):
                ref[:, j * PAIR : (j + 1) * PAIR] = jnp.dot(
                    s_ref[pl.ds(aligned(which, half), half), columns],
                    a2_ref[j],
                    preferred_element_type=F32,
                ).astype(BF16)

    width = plan.panel_window * PAIR
    mwidth = plan.merged_window * PAIR
    shape = jax.ShapeDtypeStruct((half, plan.out_blocks * PAIR), BF16)
    return pl.pallas_call(
        body,
        out_shape=[shape, shape],
        grid=(1,),
        in_specs=[SMEM, SMEM, SMEM]
        + [VMEM] * (plan.cells + 1)
        + [
            pl.BlockSpec((1, plan.range_blocks, PAIR, PAIR), lambda i: (1, 0, 0, 0)),
            pl.BlockSpec((1, plan.range_blocks, PAIR, PAIR), lambda i: (2, 0, 0, 0)),
            pl.BlockSpec((plan.merged_window, 2 * PAIR, PAIR), lambda i: (1, 0, 0)),
            VMEM,
        ],
        out_specs=[VMEM, VMEM],
        scratch_shapes=[pltpu.VMEM((plan.total_rows, width), BF16)] * 2
        + [pltpu.VMEM((plan.total_rows, mwidth), BF16)] * 2,
        compiler_params=params(),
        name="second_member",
    )(
        where,
        rng_blocks,
        ang_blocks,
        *parts,
        partial,
        rng_mats,
        rng_mats,
        ang_mats,
        last_mats,
    )


def focus(plan, where, own, other, owners, groups):
    half = plan.total_rows // 2
    columns = plan.out_blocks * TILE

    def body(where_ref, own_ref, oth_ref, owners_ref, image_ref, grad_ref):
        side = where_ref[1]
        row = lax.broadcasted_iota(jnp.int32, (half, TILE), 0) + side * half
        weight = 1.0 + 2.0 * row.astype(F32) / (plan.total_rows - 1)
        mine, theirs = [], []
        for j in range(plan.out_blocks):
            at = j * PAIR
            own_re = own_ref[:, at : at + TILE].astype(F32)
            own_im = own_ref[:, at + TILE : at + PAIR].astype(F32)
            oth_re = oth_ref[:, at : at + TILE].astype(F32)
            oth_im = oth_ref[:, at + TILE : at + PAIR].astype(F32)
            re = own_re + oth_re
            im = own_im + oth_im
            image_ref[0, :, j * TILE : (j + 1) * TILE] = re.astype(BF16)
            image_ref[1, :, j * TILE : (j + 1) * TILE] = im.astype(BF16)
            power = weight * (re * re + im * im)
            mine.append(
                jnp.sum(power * (re * own_re + im * own_im), axis=0, keepdims=True)
            )
            theirs.append(
                jnp.sum(power * (re * oth_re + im * oth_im), axis=0, keepdims=True)
            )
        mine = jnp.concatenate(mine, axis=1) / plan.total_rows
        theirs = jnp.concatenate(theirs, axis=1) / plan.total_rows
        zeroth = jnp.where(side == 0, mine, theirs)
        oneth = jnp.where(side == 0, theirs, mine)
        marks = owners_ref[...] == lax.broadcasted_iota(
            jnp.int32, (groups, columns), 0
        )
        for q, slope in ((0, zeroth), (1, oneth)):
            grad_ref[q] = jnp.sum(jnp.where(marks, slope, 0.0), axis=1, keepdims=True)

    return pl.pallas_call(
        body,
        out_shape=[
            jax.ShapeDtypeStruct((2, half, columns), BF16),
            jax.ShapeDtypeStruct((2, groups, 1), F32),
        ],
        in_specs=[SMEM, VMEM, VMEM, VMEM],
        out_specs=[VMEM, VMEM],
        compiler_params=params(),
        name="focus",
    )(where, own, other, owners)


def shards(subimages, rng_taps, rng_blocks, rng_weights, ang_taps, ang_blocks, ang_weights, owners):
    panels = lax.axis_size("panel")
    panel = lax.axis_index("panel").astype(jnp.int32)
    side = lax.axis_index("aper").astype(jnp.int32)
    groups = GRP_DEV * panels
    plan = Plan(panels, subimages.shape[2], subimages.shape[3])
    where = jnp.stack([panel, side])

    def plane_shift(step):
        return [
            (g * plan.cells + c, ((g + step) % plan.planes) * plan.cells + c)
            for g in range(plan.planes)
            for c in range(plan.cells)
        ]

    def cell_flip(flip):
        return [(i, i ^ flip) for i in range(panels)]

    sends = pack_planes(plan, where, subimages)
    windows = []
    after = None
    for pieces in sends:
        if after is not None:
            pieces, _ = lax.optimization_barrier((pieces, after))
        received = [pieces[0]] + [
            lax.ppermute(pieces[step], "panel", plane_shift(step))
            for step in range(1, plan.planes)
        ]
        after = received
        parts = pack_panels(plan, where, received)
        windows.append(
            [parts[0]]
            + [
                lax.ppermute(parts[flip], "panel", cell_flip(flip))
                for flip in range(1, plan.cells)
            ]
        )

    first = plan.merged_start(panel)
    near = first + jnp.arange(plan.merged_window, dtype=jnp.int32)
    merge_at = jnp.concatenate([near, 2 * plan.in_blocks + near])
    last_at = (
        4 * plan.in_blocks
        + panel * plan.out_blocks
        + jnp.arange(plan.out_blocks, dtype=jnp.int32)
    )
    ang_mats = build_angle(merge_at, ang_taps, ang_weights[0])
    last_mats = build_angle(last_at, ang_taps, ang_weights[0])
    rng_mats = build_range(plan, rng_taps[0], rng_weights[0])

    partial = first_member(
        plan, where, windows[0], rng_blocks[0], ang_blocks, rng_mats, ang_mats
    )
    own, send = second_member(
        plan, where, windows[1], partial, rng_blocks[0], ang_blocks, rng_mats, ang_mats, last_mats
    )
    other = lax.ppermute(send, "aper", [(0, 1), (1, 0)])
    columns = plan.out_blocks * TILE
    mine = lax.dynamic_slice_in_dim(owners[None], panel * columns, columns, 1)
    image, partials = focus(plan, where, own, other, mine, groups)
    pieces = lax.all_to_all(
        partials.reshape(2 * panels, GRP_DEV), ("aper", "panel"), 0, 0, tiled=True
    )
    return image, jnp.sum(pieces, axis=0)[None]


def solution(mesh):
    return jax.shard_map(
        shards,
        mesh=mesh,
        in_specs=(
            P(("scene", "aper"), None, "panel", None),
            P("aper", None, None),
            P("aper", None, None),
            P("aper", None, None, None, None),
            P("aper", None),
            P("aper", None),
            P("aper", None, None, None),
            P(),
        ),
        out_specs=(P(None, ("scene", "aper"), "panel"), P(("scene", "aper"), "panel")),
        check_vma=False,
    )
```

```python
import jax
import jax.numpy as jnp
from jax import lax
from jax.experimental import pallas as pl
from jax.experimental.pallas import tpu as pltpu
from jax.sharding import PartitionSpec as P

TILE = 128
PAIR = 2 * TILE
TAPS = 16
GRP_DEV = 4
F32 = jnp.float32
BF16 = jnp.bfloat16
VMEM_BYTES = 44 * 1024 * 1024


def aligned(value, step):
    return pl.multiple_of(value * step, step)


def params():
    return pltpu.CompilerParams(vmem_limit_bytes=VMEM_BYTES)


class Plan:
    def __init__(self, panels, rows, angles):
        self.panels = panels
        self.rows = rows
        self.total_rows = rows * panels
        self.in_blocks = angles // TILE
        self.own = self.in_blocks // panels
        self.cells = TILE // rows
        self.planes = panels // self.cells
        self.range_blocks = self.total_rows // TILE
        self.plane_window = min(self.cells * self.own + 4, self.in_blocks)
        self.panel_window = self.own + 4
        self.merged_window = 2 * self.own + 2
        self.out_blocks = 4 * self.own

    def plane_start(self, plane):
        return jnp.clip(
            self.cells * self.own * plane - 2, 0, self.in_blocks - self.plane_window
        )

    def panel_start(self, panel):
        return jnp.clip(self.own * panel - 2, 0, self.in_blocks - self.panel_window)

    def merged_start(self, panel):
        return jnp.clip(
            2 * self.own * panel - 1, 0, 2 * self.in_blocks - self.merged_window
        )


SMEM = pl.BlockSpec(memory_space=pltpu.SMEM)
VMEM = pl.BlockSpec(memory_space=pltpu.VMEM)
ANY = pl.BlockSpec(memory_space=pltpu.HBM)


def pack_own(plan, where, subimages):
    members = subimages.shape[0]
    others = plan.planes - 1

    def body(where_ref, x_ref, *outs):
        panel = where_ref[0]
        plane = panel // plan.cells
        cell = lax.rem(panel, plan.cells)
        for step in range(1, plan.planes):
            target = lax.rem(plane + step, plan.planes)
            column = aligned(plan.plane_start(target), TILE)
            outs[step - 1][...] = x_ref[
                :, :, :, pl.ds(column, plan.plane_window * TILE)
            ]
        for flip in range(1, plan.cells):
            target = plane * plan.cells + (cell ^ flip)
            column = aligned(plan.panel_start(target), TILE)
            outs[others + flip - 1][0] = x_ref[
                :, :, :, pl.ds(column, plan.panel_window * TILE)
            ]

    lead = (members, 2, plan.rows)
    far = jax.ShapeDtypeStruct(lead + (plan.plane_window * TILE,), BF16)
    near = jax.ShapeDtypeStruct((1,) + lead + (plan.panel_window * TILE,), BF16)
    outs = pl.pallas_call(
        body,
        out_shape=[far] * others + [near] * (plan.cells - 1),
        in_specs=[SMEM, VMEM],
        out_specs=[VMEM] * (others + plan.cells - 1),
        compiler_params=params(),
        name="pack_own",
    )(where, subimages)
    return outs[:others], outs[others:]


def pack_panels(plan, where, received):
    count = len(received)

    def body(where_ref, *refs):
        ins, outs = refs[:count], refs[count:]
        panel = where_ref[0]
        plane = panel // plan.cells
        cell = lax.rem(panel, plan.cells)
        base = plan.plane_start(plane)
        for flip in range(1, plan.cells):
            offset = plan.panel_start(plane * plan.cells + (cell ^ flip)) - base
            columns = pl.ds(aligned(offset, TILE), plan.panel_window * TILE)
            for at in range(count):
                outs[flip - 1][at] = ins[at][:, :, :, columns]

    lead = received[0].shape[:3]
    shape = jax.ShapeDtypeStruct(
        (count,) + lead + (plan.panel_window * TILE,), BF16
    )
    return pl.pallas_call(
        body,
        out_shape=[shape] * (plan.cells - 1),
        in_specs=[SMEM] + [VMEM] * count,
        out_specs=[VMEM] * (plan.cells - 1),
        compiler_params=params(),
        name="pack_panels",
    )(where, *received)


def spread_taps(base, weights):
    low = base & (TAPS - 1)
    high = base >> 4
    wide = jnp.concatenate([weights, jnp.zeros_like(weights)], axis=0)
    for bit in range(4):
        moved = pltpu.roll(wide, 1 << bit, axis=0)
        wide = jnp.where(((low >> bit) & 1) == 1, moved, wide)
    zero = jnp.zeros_like(weights)
    pieces = []
    for place in range(PAIR // TAPS):
        below = jnp.where(high == place - 1, wide[TAPS:], zero)
        pieces.append(jnp.where(high == place, wide[:TAPS], below))
    return pieces


def build_angle(blocks, taps, weights):
    count = blocks.shape[0]

    def body(blocks_ref, taps_ref, weights_ref, out_ref):
        base = taps_ref[...]
        real = spread_taps(base, weights_ref[0].astype(F32))
        imag = spread_taps(base, weights_ref[1].astype(F32))
        half = TILE // TAPS
        for place in range(PAIR // TAPS):
            row = (place // half) * PAIR + (place % half) * TAPS
            re = real[place].astype(BF16)
            im = imag[place].astype(BF16)
            neg = (-imag[place]).astype(BF16)
            out_ref[0, row : row + TAPS, :TILE] = re
            out_ref[0, row : row + TAPS, TILE:] = im
            out_ref[0, TILE + row : TILE + row + TAPS, :TILE] = neg
            out_ref[0, TILE + row : TILE + row + TAPS, TILE:] = re

    return pl.pallas_call(
        body,
        out_shape=jax.ShapeDtypeStruct((count, 2 * PAIR, PAIR), BF16),
        grid_spec=pltpu.PrefetchScalarGridSpec(
            num_scalar_prefetch=1,
            grid=(count,),
            in_specs=[
                pl.BlockSpec((1, TILE), lambda i, t: (0, t[i])),
                pl.BlockSpec((2, TAPS, TILE), lambda i, t: (0, 0, t[i])),
            ],
            out_specs=pl.BlockSpec((1, 2 * PAIR, PAIR), lambda i, t: (i, 0, 0)),
        ),
        compiler_params=params(),
        name="build_angle",
    )(blocks, taps, weights)


def build_range(plan, taps, weights):
    slots = taps.shape[0]

    def body(taps_ref, weights_ref, out_ref):
        base = taps_ref[0]
        for part in range(2):
            pieces = spread_taps(base, weights_ref[0, part].astype(F32))
            matrix = jnp.concatenate(pieces, axis=0)
            out_ref[0, 0, part * TILE : (part + 1) * TILE, :] = matrix.T.astype(BF16)

    return pl.pallas_call(
        body,
        out_shape=jax.ShapeDtypeStruct((slots, plan.range_blocks, PAIR, PAIR), BF16),
        grid=(slots, plan.range_blocks),
        in_specs=[
            pl.BlockSpec((1, 1, TILE), lambda s, j: (s, 0, j)),
            pl.BlockSpec((1, 2, TAPS, TILE), lambda s, j: (s, 0, 0, j)),
        ],
        out_specs=pl.BlockSpec((1, 1, PAIR, PAIR), lambda s, j: (s, j, 0, 0)),
        compiler_params=params(),
        name="build_range",
    )(taps.reshape(slots, 1, -1), weights)


def range_step(plan, starts, matrix, source, target, blocks):
    for j in range(plan.range_blocks):
        rows = pl.ds(aligned(starts(j), TILE), PAIR)
        out = slice(j * TILE, (j + 1) * TILE)
        for block in range(0, blocks, 2):
            count = min(2, blocks - block)
            of_real, of_imag = [
                jnp.dot(
                    matrix(j), source(part, rows, block, count), preferred_element_type=F32
                )
                for part in range(2)
            ]
            real = (of_real[:TILE] - of_imag[TILE:]).astype(BF16)
            imag = (of_real[TILE:] + of_imag[:TILE]).astype(BF16)
            for at in range(count):
                lane = (block + at) * PAIR
                piece = slice(at * TILE, (at + 1) * TILE)
                target[out, lane : lane + TILE] = real[:, piece]
                target[out, lane + TILE : lane + PAIR] = imag[:, piece]


def merge(plan, where, groups, parts, held, rng_blocks, ang_blocks, rng_mats, ang_mats, last_mats):
    half = plan.total_rows // 2
    members = 2
    cells, planes = plan.cells, plan.planes
    width = plan.panel_window
    mwidth = plan.merged_window
    flips = cells - 1
    n_parts = flips * len(groups)
    n_in = n_parts + planes
    flat = [part for per_flip in parts for part in per_flip] + list(held)

    def body(where_ref, rb_ref, ab_ref, *refs):
        ins = refs[:n_in]
        rm_hbm, am_hbm, a2_hbm, own_ref, send_ref = refs[n_in : n_in + 5]
        x_ref, z_ref, y_ref, s_ref, rm_ref, am_ref, a2_ref, sem, wsem = refs[n_in + 5 :]
        panel = where_ref[0]
        side = where_ref[1]
        plane = panel // cells
        cell = lax.rem(panel, cells)
        loads = [[] for _ in range(members)]
        own_at = plan.panel_start(panel)
        for member in range(members):
            for gi, group in enumerate(groups):
                for at, step in enumerate(group):
                    source = lax.rem(plane + planes - step, planes)
                    for flip in range(cells):
                        row = aligned(source * cells + (cell ^ flip), plan.rows)
                        column = own_at - (plan.plane_start(plane) if step else 0)
                        columns = pl.ds(aligned(column, TILE), width * TILE)
                        loads[member].append(
                            pltpu.make_async_copy(
                                ins[gi * flips + flip - 1].at[at, member]
                                if flip
                                else ins[n_parts + step].at[member, :, :, columns],
                                x_ref.at[member, :, pl.ds(row, plan.rows), :],
                                sem.at[member, len(loads[member])],
                            )
                        )
        weights = [
            pltpu.make_async_copy(src, dst, wsem.at[i])
            for i, (src, dst) in enumerate(
                ((rm_hbm, rm_ref), (am_hbm, am_ref), (a2_hbm, a2_ref))
            )
        ]
        weights[0].start()
        for member in range(members):
            for load in loads[member]:
                load.start()
        weights[1].start()
        weights[2].start()
        weights[0].wait()
        for member in range(members):
            for load in loads[member]:
                load.wait()
            range_step(
                plan,
                lambda j: rb_ref[member, j],
                lambda j: rm_ref[member, j],
                lambda part, rows, block, count: x_ref[
                    member, part, rows, block * TILE : (block + count) * TILE
                ],
                z_ref.at[member],
                width,
            )
        first = plan.merged_start(panel)
        base = plan.panel_start(panel)
        weights[1].wait()
        for j in range(mwidth):
            terms = []
            for member in range(members):
                start = ab_ref[0, 2 * plan.in_blocks * member + first + j] - base
                terms.append(
                    jnp.dot(
                        z_ref[member, :, pl.ds(aligned(start, PAIR), 2 * PAIR)],
                        am_ref[member * mwidth + j],
                        preferred_element_type=F32,
                    )
                )
            total = (terms[0] + terms[1]).astype(BF16)
            for part in range(2):
                y_ref[part, :, j * TILE : (j + 1) * TILE] = total[
                    :, part * TILE : (part + 1) * TILE
                ]
        range_step(
            plan,
            lambda j: rb_ref[2, j],
            lambda j: rm_ref[2, j],
            lambda part, rows, block, count: y_ref[
                part, rows, block * TILE : (block + count) * TILE
            ],
            s_ref,
            mwidth,
        )
        weights[2].wait()
        for which, ref in ((1 - side, send_ref), (side, own_ref)):
            for j in range(plan.out_blocks):
                place = 4 * plan.in_blocks + panel * plan.out_blocks + j
                columns = pl.ds(aligned(ab_ref[0, place] - first, PAIR), 2 * PAIR)
                ref[:, j * PAIR : (j + 1) * PAIR] = jnp.dot(
                    s_ref[pl.ds(aligned(which, half), half), columns],
                    a2_ref[j],
                    preferred_element_type=F32,
                ).astype(BF16)

    shape = jax.ShapeDtypeStruct((half, plan.out_blocks * PAIR), BF16)
    rows = plan.total_rows
    return pl.pallas_call(
        body,
        out_shape=[shape, shape],
        in_specs=[SMEM, SMEM, SMEM] + [ANY] * (n_in + 3),
        out_specs=[VMEM, VMEM],
        scratch_shapes=[
            pltpu.VMEM((members, 2, rows, width * TILE), BF16),
            pltpu.VMEM((members, rows, width * PAIR), BF16),
            pltpu.VMEM((2, rows, mwidth * TILE), BF16),
            pltpu.VMEM((rows, mwidth * PAIR), BF16),
            pltpu.VMEM(rng_mats.shape, BF16),
            pltpu.VMEM(ang_mats.shape, BF16),
            pltpu.VMEM(last_mats.shape, BF16),
            pltpu.SemaphoreType.DMA((members, cells * planes)),
            pltpu.SemaphoreType.DMA((3,)),
        ],
        compiler_params=params(),
        name="merge",
    )(where, rng_blocks, ang_blocks, *flat, rng_mats, ang_mats, last_mats)


def focus(plan, where, own, other, owners, groups):
    half = plan.total_rows // 2
    columns = plan.out_blocks * TILE

    def body(where_ref, own_ref, oth_ref, owners_ref, image_ref, grad_ref):
        side = where_ref[1]
        row = lax.broadcasted_iota(jnp.int32, (half, TILE), 0) + side * half
        weight = 1.0 + 2.0 * row.astype(F32) / (plan.total_rows - 1)
        mine, theirs = [], []
        for j in range(plan.out_blocks):
            at = j * PAIR
            own_re = own_ref[:, at : at + TILE].astype(F32)
            own_im = own_ref[:, at + TILE : at + PAIR].astype(F32)
            oth_re = oth_ref[:, at : at + TILE].astype(F32)
            oth_im = oth_ref[:, at + TILE : at + PAIR].astype(F32)
            re = own_re + oth_re
            im = own_im + oth_im
            image_ref[0, :, j * TILE : (j + 1) * TILE] = re.astype(BF16)
            image_ref[1, :, j * TILE : (j + 1) * TILE] = im.astype(BF16)
            power = weight * (re * re + im * im)
            mine.append(
                jnp.sum(power * (re * own_re + im * own_im), axis=0, keepdims=True)
            )
            theirs.append(
                jnp.sum(power * (re * oth_re + im * oth_im), axis=0, keepdims=True)
            )
        mine = jnp.concatenate(mine, axis=1) / plan.total_rows
        theirs = jnp.concatenate(theirs, axis=1) / plan.total_rows
        zeroth = jnp.where(side == 0, mine, theirs)
        oneth = jnp.where(side == 0, theirs, mine)
        marks = owners_ref[...] == lax.broadcasted_iota(
            jnp.int32, (groups, columns), 0
        )
        for q, slope in ((0, zeroth), (1, oneth)):
            grad_ref[q] = jnp.sum(jnp.where(marks, slope, 0.0), axis=1, keepdims=True)

    return pl.pallas_call(
        body,
        out_shape=[
            jax.ShapeDtypeStruct((2, half, columns), BF16),
            jax.ShapeDtypeStruct((2, groups, 1), F32),
        ],
        in_specs=[SMEM, VMEM, VMEM, VMEM],
        out_specs=[VMEM, VMEM],
        compiler_params=params(),
        name="focus",
    )(where, own, other, owners)


def shards(subimages, rng_taps, rng_blocks, rng_weights, ang_taps, ang_blocks, ang_weights, owners):
    panels = lax.axis_size("panel")
    panel = lax.axis_index("panel").astype(jnp.int32)
    side = lax.axis_index("aper").astype(jnp.int32)
    groups = GRP_DEV * panels
    plan = Plan(panels, subimages.shape[2], subimages.shape[3])
    where = jnp.stack([panel, side])

    def plane_shift(step):
        return [
            (g * plan.cells + c, ((g + step) % plan.planes) * plan.cells + c)
            for g in range(plan.planes)
            for c in range(plan.cells)
        ]

    def cell_flip(flip):
        return [(i, i ^ flip) for i in range(panels)]

    steps = [
        sorted({step, plan.planes - step}) for step in range(1, plan.planes // 2 + 1)
    ]
    order = [[0]] + steps
    far, near_parts = pack_own(plan, where, subimages)

    def across(pieces):
        return [
            lax.ppermute(pieces[flip - 1], "panel", cell_flip(flip))
            for flip in range(1, plan.cells)
        ]

    parts = []
    held = {0: subimages}
    packed = near_parts
    arrived = {
        step: lax.ppermute(far[step - 1], "panel", plane_shift(step))
        for group in steps
        for step in group
    }
    for group in steps:
        received = [arrived[step] for step in group]
        parts.append(across(packed))
        parts, received = lax.optimization_barrier((parts, received))
        held.update(zip(group, received))
        packed = pack_panels(plan, where, received)
    parts.append(across(packed))
    held = [held[step] for step in range(plan.planes)]

    first = plan.merged_start(panel)
    near = first + jnp.arange(plan.merged_window, dtype=jnp.int32)
    merge_at = jnp.concatenate([near, 2 * plan.in_blocks + near])
    last_at = (
        4 * plan.in_blocks
        + panel * plan.out_blocks
        + jnp.arange(plan.out_blocks, dtype=jnp.int32)
    )
    ang_mats = build_angle(merge_at, ang_taps, ang_weights[0])
    last_mats = build_angle(last_at, ang_taps, ang_weights[0])
    rng_mats = build_range(plan, rng_taps[0], rng_weights[0])

    own, send = merge(
        plan, where, order, parts, held, rng_blocks[0], ang_blocks, rng_mats, ang_mats, last_mats
    )
    other = lax.ppermute(send, "aper", [(0, 1), (1, 0)])
    columns = plan.out_blocks * TILE
    mine = lax.dynamic_slice_in_dim(owners[None], panel * columns, columns, 1)
    image, partials = focus(plan, where, own, other, mine, groups)
    pieces = lax.all_to_all(
        partials.reshape(2 * panels, GRP_DEV), ("aper", "panel"), 0, 0, tiled=True
    )
    return image, jnp.sum(pieces, axis=0)[None]


def solution(mesh):
    return jax.shard_map(
        shards,
        mesh=mesh,
        in_specs=(
            P(("scene", "aper"), None, "panel", None),
            P("aper", None, None),
            P("aper", None, None),
            P("aper", None, None, None, None),
            P("aper", None),
            P("aper", None),
            P("aper", None, None, None),
            P(),
        ),
        out_specs=(P(None, ("scene", "aper"), "panel"), P(("scene", "aper"), "panel")),
        check_vma=False,
    )
```

```python
import jax
import jax.numpy as jnp
from jax import lax
from jax.experimental import pallas as pl
from jax.experimental.pallas import tpu as pltpu
from jax.sharding import PartitionSpec as P

TILE = 128
PAIR = 2 * TILE
TAPS = 16
GRP_DEV = 4
STRIP = 32
F32 = jnp.float32
BF16 = jnp.bfloat16
VMEM_BYTES = 44 * 1024 * 1024


def aligned(value, step):
    return pl.multiple_of(value * step, step)


def params():
    return pltpu.CompilerParams(vmem_limit_bytes=VMEM_BYTES)


class Plan:
    def __init__(self, panels, rows, angles):
        self.panels = panels
        self.rows = rows
        self.total_rows = rows * panels
        self.in_blocks = angles // TILE
        self.own = self.in_blocks // panels
        self.cells = TILE // rows
        self.planes = panels // self.cells
        self.range_blocks = self.total_rows // TILE
        self.plane_window = min(self.cells * self.own + 4, self.in_blocks)
        self.panel_window = self.own + 4
        self.merged_window = 2 * self.own + 2
        self.out_blocks = 4 * self.own

    def plane_start(self, plane):
        return jnp.clip(
            self.cells * self.own * plane - 2, 0, self.in_blocks - self.plane_window
        )

    def panel_start(self, panel):
        return jnp.clip(self.own * panel - 2, 0, self.in_blocks - self.panel_window)

    def merged_start(self, panel):
        return jnp.clip(
            2 * self.own * panel - 1, 0, 2 * self.in_blocks - self.merged_window
        )


SMEM = pl.BlockSpec(memory_space=pltpu.SMEM)
VMEM = pl.BlockSpec(memory_space=pltpu.VMEM)
ANY = pl.BlockSpec(memory_space=pl.ANY)


def pack_own(plan, where, subimages):
    members = subimages.shape[0]
    others = plan.planes - 1

    def body(where_ref, x_ref, *outs):
        panel = where_ref[0]
        plane = panel // plan.cells
        cell = lax.rem(panel, plan.cells)
        for step in range(1, plan.planes):
            target = lax.rem(plane + step, plan.planes)
            column = aligned(plan.plane_start(target), TILE)
            outs[step - 1][...] = x_ref[
                :, :, :, pl.ds(column, plan.plane_window * TILE)
            ]
        for flip in range(1, plan.cells):
            target = plane * plan.cells + (cell ^ flip)
            column = aligned(plan.panel_start(target), TILE)
            outs[others + flip - 1][0] = x_ref[
                :, :, :, pl.ds(column, plan.panel_window * TILE)
            ]

    lead = (members, 2, plan.rows)
    far = jax.ShapeDtypeStruct(lead + (plan.plane_window * TILE,), BF16)
    near = jax.ShapeDtypeStruct((1,) + lead + (plan.panel_window * TILE,), BF16)
    outs = pl.pallas_call(
        body,
        out_shape=[far] * others + [near] * (plan.cells - 1),
        in_specs=[SMEM, VMEM],
        out_specs=[VMEM] * (others + plan.cells - 1),
        compiler_params=params(),
        name="pack_own",
    )(where, subimages)
    return outs[:others], outs[others:]


def pack_panels(plan, where, received):
    count = len(received)

    def body(where_ref, *refs):
        ins, outs = refs[:count], refs[count:]
        panel = where_ref[0]
        plane = panel // plan.cells
        cell = lax.rem(panel, plan.cells)
        base = plan.plane_start(plane)
        for flip in range(1, plan.cells):
            offset = plan.panel_start(plane * plan.cells + (cell ^ flip)) - base
            columns = pl.ds(aligned(offset, TILE), plan.panel_window * TILE)
            for at in range(count):
                outs[flip - 1][at] = ins[at][:, :, :, columns]

    lead = received[0].shape[:3]
    shape = jax.ShapeDtypeStruct(
        (count,) + lead + (plan.panel_window * TILE,), BF16
    )
    return pl.pallas_call(
        body,
        out_shape=[shape] * (plan.cells - 1),
        in_specs=[SMEM] + [VMEM] * count,
        out_specs=[VMEM] * (plan.cells - 1),
        compiler_params=params(),
        name="pack_panels",
    )(where, *received)


def spread_taps(base, weights):
    low = base & (TAPS - 1)
    high = base >> 4
    wide = jnp.concatenate([weights, jnp.zeros_like(weights)], axis=0)
    for bit in range(4):
        moved = pltpu.roll(wide, 1 << bit, axis=0)
        wide = jnp.where(((low >> bit) & 1) == 1, moved, wide)
    zero = jnp.zeros_like(weights)
    pieces = []
    for place in range(PAIR // TAPS):
        below = jnp.where(high == place - 1, wide[TAPS:], zero)
        pieces.append(jnp.where(high == place, wide[:TAPS], below))
    return pieces


def build_angle(blocks, taps, weights):
    count = blocks.shape[0]

    def body(blocks_ref, taps_ref, weights_ref, out_ref):
        base = taps_ref[...]
        real = spread_taps(base, weights_ref[0].astype(F32))
        imag = spread_taps(base, weights_ref[1].astype(F32))
        half = TILE // TAPS
        for place in range(PAIR // TAPS):
            row = (place // half) * PAIR + (place % half) * TAPS
            re = real[place].astype(BF16)
            im = imag[place].astype(BF16)
            neg = (-imag[place]).astype(BF16)
            out_ref[0, row : row + TAPS, :TILE] = re
            out_ref[0, row : row + TAPS, TILE:] = im
            out_ref[0, TILE + row : TILE + row + TAPS, :TILE] = neg
            out_ref[0, TILE + row : TILE + row + TAPS, TILE:] = re

    return pl.pallas_call(
        body,
        out_shape=jax.ShapeDtypeStruct((count, 2 * PAIR, PAIR), BF16),
        grid_spec=pltpu.PrefetchScalarGridSpec(
            num_scalar_prefetch=1,
            grid=(count,),
            in_specs=[
                pl.BlockSpec((1, TILE), lambda i, t: (0, t[i])),
                pl.BlockSpec((2, TAPS, TILE), lambda i, t: (0, 0, t[i])),
            ],
            out_specs=pl.BlockSpec((1, 2 * PAIR, PAIR), lambda i, t: (i, 0, 0)),
        ),
        compiler_params=params(),
        name="build_angle",
    )(blocks, taps, weights)


def build_range(plan, taps, weights):
    slots = taps.shape[0]

    def body(taps_ref, weights_ref, out_ref):
        base = taps_ref[0]
        for part in range(2):
            pieces = spread_taps(base, weights_ref[0, part].astype(F32))
            matrix = jnp.concatenate(pieces, axis=0)
            out_ref[0, 0, part * TILE : (part + 1) * TILE, :] = matrix.T.astype(BF16)

    return pl.pallas_call(
        body,
        out_shape=jax.ShapeDtypeStruct((slots, plan.range_blocks, PAIR, PAIR), BF16),
        grid=(slots, plan.range_blocks),
        in_specs=[
            pl.BlockSpec((1, 1, TILE), lambda s, j: (s, 0, j)),
            pl.BlockSpec((1, 2, TAPS, TILE), lambda s, j: (s, 0, 0, j)),
        ],
        out_specs=pl.BlockSpec((1, 1, PAIR, PAIR), lambda s, j: (s, j, 0, 0)),
        compiler_params=params(),
        name="build_range",
    )(taps.reshape(slots, 1, -1), weights)


def range_step(plan, starts, matrix, source, target, blocks):
    for j in range(plan.range_blocks):
        rows = pl.ds(aligned(starts(j), TILE), PAIR)
        out = slice(j * TILE, (j + 1) * TILE)
        for block in range(0, blocks, 2):
            count = min(2, blocks - block)
            of_real, of_imag = [
                jnp.dot(
                    matrix(j), source(part, rows, block, count), preferred_element_type=F32
                )
                for part in range(2)
            ]
            real = (of_real[:TILE] - of_imag[TILE:]).astype(BF16)
            imag = (of_real[TILE:] + of_imag[:TILE]).astype(BF16)
            for at in range(count):
                lane = (block + at) * PAIR
                piece = slice(at * TILE, (at + 1) * TILE)
                target[out, lane : lane + TILE] = real[:, piece]
                target[out, lane + TILE : lane + PAIR] = imag[:, piece]


def merge(plan, where, groups, parts, held, rng_blocks, ang_blocks, rng_mats, ang_mats, last_mats):
    half = plan.total_rows // 2
    members = 2
    cells, planes = plan.cells, plan.planes
    width = plan.panel_window
    mwidth = plan.merged_window
    flips = cells - 1
    n_parts = flips * len(groups)
    n_in = n_parts + planes
    flat = [part for per_flip in parts for part in per_flip] + list(held)

    def body(where_ref, rb_ref, ab_ref, *refs):
        ins = refs[:n_in]
        rm_hbm, am_hbm, a2_hbm, own_ref, send_ref = refs[n_in : n_in + 5]
        x_ref, z_ref, y_ref, s_ref, rm_ref, am_ref, a2_ref, sem, wsem = refs[n_in + 5 :]
        panel = where_ref[0]
        side = where_ref[1]
        plane = panel // cells
        cell = lax.rem(panel, cells)
        own_at = plan.panel_start(panel)
        loads = []
        for step in range(planes):
            row = aligned(lax.rem(plane + planes - step, planes) * cells + cell, plan.rows)
            column = own_at - (plan.plane_start(plane) if step else 0)
            loads.append(
                pltpu.make_async_copy(
                    ins[n_parts + step].at[
                        :, :, :, pl.ds(aligned(column, TILE), width * TILE)
                    ],
                    x_ref.at[:, :, pl.ds(row, plan.rows), :],
                    sem.at[step],
                )
            )
        weights = [
            pltpu.make_async_copy(rm_hbm.at[slot], rm_ref.at[slot], wsem.at[slot])
            for slot in range(3)
        ] + [
            pltpu.make_async_copy(am_hbm, am_ref, wsem.at[3]),
            pltpu.make_async_copy(a2_hbm, a2_ref, wsem.at[4]),
        ]
        weights[0].start()
        for load in loads:
            load.start()
        for at in (1, 3, 2, 4):
            weights[at].start()
        for load in loads:
            load.wait()
        for member in range(members):
            for gi, group in enumerate(groups):
                for at, step in enumerate(group):
                    source = lax.rem(plane + planes - step, planes) * cells
                    for flip in range(1, cells):
                        rows = pl.ds(aligned(source + (cell ^ flip), plan.rows), plan.rows)
                        x_ref[member, :, rows, :] = ins[gi * flips + flip - 1][at, member]
            weights[member].wait()
            range_step(
                plan,
                lambda j: rb_ref[member, j],
                lambda j: rm_ref[member, j],
                lambda part, rows, block, count: x_ref[
                    member, part, rows, block * TILE : (block + count) * TILE
                ],
                z_ref.at[member],
                width,
            )
        first = plan.merged_start(panel)
        base = plan.panel_start(panel)
        weights[3].wait()
        for j in range(mwidth):
            terms = []
            for member in range(members):
                start = ab_ref[0, 2 * plan.in_blocks * member + first + j] - base
                terms.append(
                    jnp.dot(
                        z_ref[member, :, pl.ds(aligned(start, PAIR), 2 * PAIR)],
                        am_ref[member * mwidth + j],
                        preferred_element_type=F32,
                    )
                )
            total = (terms[0] + terms[1]).astype(BF16)
            for part in range(2):
                y_ref[part, :, j * TILE : (j + 1) * TILE] = total[
                    :, part * TILE : (part + 1) * TILE
                ]
        weights[2].wait()
        range_step(
            plan,
            lambda j: rb_ref[2, j],
            lambda j: rm_ref[2, j],
            lambda part, rows, block, count: y_ref[
                part, rows, block * TILE : (block + count) * TILE
            ],
            s_ref,
            mwidth,
        )
        weights[4].wait()
        for which, ref in ((1 - side, send_ref), (side, own_ref)):
            for j in range(plan.out_blocks):
                place = 4 * plan.in_blocks + panel * plan.out_blocks + j
                columns = pl.ds(aligned(ab_ref[0, place] - first, PAIR), 2 * PAIR)
                ref[:, j * PAIR : (j + 1) * PAIR] = jnp.dot(
                    s_ref[pl.ds(aligned(which, half), half), columns],
                    a2_ref[j],
                    preferred_element_type=F32,
                ).astype(BF16)

    shape = jax.ShapeDtypeStruct((half, plan.out_blocks * PAIR), BF16)
    rows = plan.total_rows
    return pl.pallas_call(
        body,
        out_shape=[shape, shape],
        in_specs=[SMEM, SMEM, SMEM] + [VMEM] * n_parts + [ANY] * (planes + 3),
        out_specs=[VMEM, VMEM],
        scratch_shapes=[
            pltpu.VMEM((members, 2, rows, width * TILE), BF16),
            pltpu.VMEM((members, rows, width * PAIR), BF16),
            pltpu.VMEM((2, rows, mwidth * TILE), BF16),
            pltpu.VMEM((rows, mwidth * PAIR), BF16),
            pltpu.VMEM(rng_mats.shape, BF16),
            pltpu.VMEM(ang_mats.shape, BF16),
            pltpu.VMEM(last_mats.shape, BF16),
            pltpu.SemaphoreType.DMA((planes,)),
            pltpu.SemaphoreType.DMA((5,)),
        ],
        compiler_params=params(),
        name="merge",
    )(where, rng_blocks, ang_blocks, *flat, rng_mats, ang_mats, last_mats)


def focus(plan, where, own, other, owners, groups):
    half = plan.total_rows // 2
    columns = plan.out_blocks * TILE

    def body(
        where_ref, own_ref, oth_ref, owners_ref, image_ref, grad_ref, held_ref, sem
    ):
        side = where_ref[1]
        row = lax.broadcasted_iota(jnp.int32, (STRIP, TILE), 0) + side * half
        mine, theirs = [], []
        stores = []
        for j in range(plan.out_blocks):
            at = j * PAIR
            sums = [jnp.zeros((8, TILE), F32)] * 2
            for top in range(0, half, STRIP):
                strip = slice(top, top + STRIP)
                weight = 1.0 + 2.0 * (row + top).astype(F32) / (plan.total_rows - 1)
                own_re = own_ref[strip, at : at + TILE].astype(F32)
                own_im = own_ref[strip, at + TILE : at + PAIR].astype(F32)
                oth_re = oth_ref[strip, at : at + TILE].astype(F32)
                oth_im = oth_ref[strip, at + TILE : at + PAIR].astype(F32)
                re = own_re + oth_re
                im = own_im + oth_im
                held_ref[0, strip, j * TILE : (j + 1) * TILE] = re.astype(BF16)
                held_ref[1, strip, j * TILE : (j + 1) * TILE] = im.astype(BF16)
                power = weight * (re * re + im * im)
                for which, (a, b) in enumerate(((own_re, own_im), (oth_re, oth_im))):
                    term = power * (re * a + im * b)
                    sums[which] = sums[which] + jnp.sum(
                        term.reshape(STRIP // 8, 8, TILE), axis=0
                    )
            stores.append(
                pltpu.make_async_copy(
                    held_ref.at[:, :, j * TILE : (j + 1) * TILE],
                    image_ref.at[:, :, j * TILE : (j + 1) * TILE],
                    sem.at[j],
                )
            )
            stores[-1].start()
            mine.append(jnp.sum(sums[0], axis=0, keepdims=True))
            theirs.append(jnp.sum(sums[1], axis=0, keepdims=True))
        mine = jnp.concatenate(mine, axis=1) / plan.total_rows
        theirs = jnp.concatenate(theirs, axis=1) / plan.total_rows
        zeroth = jnp.where(side == 0, mine, theirs)
        oneth = jnp.where(side == 0, theirs, mine)
        marks = owners_ref[...] == lax.broadcasted_iota(
            jnp.int32, (groups, columns), 0
        )
        for q, slope in ((0, zeroth), (1, oneth)):
            grad_ref[q] = jnp.sum(jnp.where(marks, slope, 0.0), axis=1, keepdims=True)
        for store in stores:
            store.wait()

    return pl.pallas_call(
        body,
        out_shape=[
            jax.ShapeDtypeStruct((2, half, columns), BF16),
            jax.ShapeDtypeStruct((2, groups, 1), F32),
        ],
        in_specs=[SMEM, VMEM, VMEM, VMEM],
        out_specs=[ANY, VMEM],
        scratch_shapes=[
            pltpu.VMEM((2, half, columns), BF16),
            pltpu.SemaphoreType.DMA((plan.out_blocks,)),
        ],
        compiler_params=params(),
        name="focus",
    )(where, own, other, owners)


def shards(subimages, rng_taps, rng_blocks, rng_weights, ang_taps, ang_blocks, ang_weights, owners):
    panels = lax.axis_size("panel")
    panel = lax.axis_index("panel").astype(jnp.int32)
    side = lax.axis_index("aper").astype(jnp.int32)
    groups = GRP_DEV * panels
    plan = Plan(panels, subimages.shape[2], subimages.shape[3])
    where = jnp.stack([panel, side])

    def plane_shift(step):
        return [
            (g * plan.cells + c, ((g + step) % plan.planes) * plan.cells + c)
            for g in range(plan.planes)
            for c in range(plan.cells)
        ]

    def cell_flip(flip):
        return [(i, i ^ flip) for i in range(panels)]

    steps = [
        sorted({step, plan.planes - step}) for step in range(1, plan.planes // 2 + 1)
    ]
    order = [[0]] + steps
    far, near_parts = pack_own(plan, where, subimages)

    def across(pieces):
        return [
            lax.ppermute(pieces[flip - 1], "panel", cell_flip(flip))
            for flip in range(1, plan.cells)
        ]

    parts = []
    held = {0: subimages}
    packed = near_parts
    arrived = {
        step: lax.ppermute(far[step - 1], "panel", plane_shift(step))
        for group in steps
        for step in group
    }
    for group in steps:
        received = [arrived[step] for step in group]
        parts.append(across(packed))
        tied = [parts[-1][0]] if len(parts) > 1 else parts[-1]
        tied, received = lax.optimization_barrier((tied, received))
        parts[-1][: len(tied)] = tied
        held.update(zip(group, received))
        packed = pack_panels(plan, where, received)
    parts.append(across(packed))
    held = [held[step] for step in range(plan.planes)]

    first = plan.merged_start(panel)
    near = first + jnp.arange(plan.merged_window, dtype=jnp.int32)
    merge_at = jnp.concatenate([near, 2 * plan.in_blocks + near])
    last_at = (
        4 * plan.in_blocks
        + panel * plan.out_blocks
        + jnp.arange(plan.out_blocks, dtype=jnp.int32)
    )
    ang_mats = build_angle(merge_at, ang_taps, ang_weights[0])
    last_mats = build_angle(last_at, ang_taps, ang_weights[0])
    rng_mats = build_range(plan, rng_taps[0], rng_weights[0])

    own, send = merge(
        plan, where, order, parts, held, rng_blocks[0], ang_blocks, rng_mats, ang_mats, last_mats
    )
    other = lax.ppermute(send, "aper", [(0, 1), (1, 0)])
    columns = plan.out_blocks * TILE
    mine = lax.dynamic_slice_in_dim(owners[None], panel * columns, columns, 1)
    image, partials = focus(plan, where, own, other, mine, groups)
    pieces = lax.all_to_all(
        partials.reshape(2 * panels, GRP_DEV), ("aper", "panel"), 0, 0, tiled=True
    )
    return image, jnp.sum(pieces, axis=0)[None]


def solution(mesh):
    return jax.shard_map(
        shards,
        mesh=mesh,
        in_specs=(
            P(("scene", "aper"), None, "panel", None),
            P("aper", None, None),
            P("aper", None, None),
            P("aper", None, None, None, None),
            P("aper", None),
            P("aper", None),
            P("aper", None, None, None),
            P(),
        ),
        out_specs=(P(None, ("scene", "aper"), "panel"), P(("scene", "aper"), "panel")),
        check_vma=False,
    )
```

```python
import jax
import jax.numpy as jnp
from jax import lax
from jax.experimental import pallas as pl
from jax.experimental.pallas import tpu as pltpu
from jax.sharding import PartitionSpec as P

TILE = 128
PAIR = 2 * TILE
TAPS = 16
GRP_DEV = 4
STRIP = 32
F32 = jnp.float32
BF16 = jnp.bfloat16
VMEM_BYTES = 44 * 1024 * 1024


def aligned(value, step):
    return pl.multiple_of(value * step, step)


def params():
    return pltpu.CompilerParams(vmem_limit_bytes=VMEM_BYTES)


class Plan:
    def __init__(self, panels, rows, angles):
        self.panels = panels
        self.rows = rows
        self.total_rows = rows * panels
        self.in_blocks = angles // TILE
        self.own = self.in_blocks // panels
        self.cells = TILE // rows
        self.planes = panels // self.cells
        self.range_blocks = self.total_rows // TILE
        self.plane_window = min(self.cells * self.own + 4, self.in_blocks)
        self.panel_window = self.own + 4
        self.merged_window = 2 * self.own + 2
        self.out_blocks = 4 * self.own

    def plane_start(self, plane):
        return jnp.clip(
            self.cells * self.own * plane - 2, 0, self.in_blocks - self.plane_window
        )

    def panel_start(self, panel):
        return jnp.clip(self.own * panel - 2, 0, self.in_blocks - self.panel_window)

    def merged_start(self, panel):
        return jnp.clip(
            2 * self.own * panel - 1, 0, 2 * self.in_blocks - self.merged_window
        )


SMEM = pl.BlockSpec(memory_space=pltpu.SMEM)
VMEM = pl.BlockSpec(memory_space=pltpu.VMEM)
ANY = pl.BlockSpec(memory_space=pl.ANY)


def pack_own(plan, where, subimages, steps, flips):
    members = subimages.shape[0]
    others = len(steps)

    def body(where_ref, x_ref, *outs):
        panel = where_ref[0]
        plane = panel // plan.cells
        cell = lax.rem(panel, plan.cells)
        for at, step in enumerate(steps):
            target = lax.rem(plane + step, plan.planes)
            column = aligned(plan.plane_start(target), TILE)
            outs[at][...] = x_ref[:, :, :, pl.ds(column, plan.plane_window * TILE)]
        for at, flip in enumerate(flips):
            target = plane * plan.cells + (cell ^ flip)
            column = aligned(plan.panel_start(target), TILE)
            outs[others + at][0] = x_ref[:, :, :, pl.ds(column, plan.panel_window * TILE)]

    lead = (members, 2, plan.rows)
    far = jax.ShapeDtypeStruct(lead + (plan.plane_window * TILE,), BF16)
    near = jax.ShapeDtypeStruct((1,) + lead + (plan.panel_window * TILE,), BF16)
    outs = pl.pallas_call(
        body,
        out_shape=[far] * others + [near] * len(flips),
        in_specs=[SMEM, VMEM],
        out_specs=[VMEM] * (others + len(flips)),
        compiler_params=params(),
        name="pack_own",
    )(where, subimages)
    return outs[:others], outs[others:]


def pack_panels(plan, where, received):
    count = len(received)

    def body(where_ref, *refs):
        ins, outs = refs[:count], refs[count:]
        panel = where_ref[0]
        plane = panel // plan.cells
        cell = lax.rem(panel, plan.cells)
        base = plan.plane_start(plane)
        for flip in range(1, plan.cells):
            offset = plan.panel_start(plane * plan.cells + (cell ^ flip)) - base
            columns = pl.ds(aligned(offset, TILE), plan.panel_window * TILE)
            for at in range(count):
                outs[flip - 1][at] = ins[at][:, :, :, columns]

    lead = received[0].shape[:3]
    shape = jax.ShapeDtypeStruct(
        (count,) + lead + (plan.panel_window * TILE,), BF16
    )
    return pl.pallas_call(
        body,
        out_shape=[shape] * (plan.cells - 1),
        in_specs=[SMEM] + [VMEM] * count,
        out_specs=[VMEM] * (plan.cells - 1),
        compiler_params=params(),
        name="pack_panels",
    )(where, *received)


def spread_taps(base, weights):
    low = base & (TAPS - 1)
    high = base >> 4
    wide = jnp.concatenate([weights, jnp.zeros_like(weights)], axis=0)
    for bit in range(4):
        moved = pltpu.roll(wide, 1 << bit, axis=0)
        wide = jnp.where(((low >> bit) & 1) == 1, moved, wide)
    zero = jnp.zeros_like(weights)
    pieces = []
    for place in range(PAIR // TAPS):
        below = jnp.where(high == place - 1, wide[TAPS:], zero)
        pieces.append(jnp.where(high == place, wide[:TAPS], below))
    return pieces


def build_angle(blocks, taps, weights):
    count = blocks.shape[0]

    def body(blocks_ref, taps_ref, weights_ref, out_ref):
        base = taps_ref[...]
        real = spread_taps(base, weights_ref[0].astype(F32))
        imag = spread_taps(base, weights_ref[1].astype(F32))
        half = TILE // TAPS
        for place in range(PAIR // TAPS):
            row = (place // half) * PAIR + (place % half) * TAPS
            re = real[place].astype(BF16)
            im = imag[place].astype(BF16)
            neg = (-imag[place]).astype(BF16)
            out_ref[0, row : row + TAPS, :TILE] = re
            out_ref[0, row : row + TAPS, TILE:] = im
            out_ref[0, TILE + row : TILE + row + TAPS, :TILE] = neg
            out_ref[0, TILE + row : TILE + row + TAPS, TILE:] = re

    return pl.pallas_call(
        body,
        out_shape=jax.ShapeDtypeStruct((count, 2 * PAIR, PAIR), BF16),
        grid_spec=pltpu.PrefetchScalarGridSpec(
            num_scalar_prefetch=1,
            grid=(count,),
            in_specs=[
                pl.BlockSpec((1, TILE), lambda i, t: (0, t[i])),
                pl.BlockSpec((2, TAPS, TILE), lambda i, t: (0, 0, t[i])),
            ],
            out_specs=pl.BlockSpec((1, 2 * PAIR, PAIR), lambda i, t: (i, 0, 0)),
        ),
        compiler_params=params(),
        name="build_angle",
    )(blocks, taps, weights)


def build_range(plan, taps, weights):
    slots = taps.shape[0]

    def body(taps_ref, weights_ref, out_ref):
        base = taps_ref[0]
        for part in range(2):
            pieces = spread_taps(base, weights_ref[0, part].astype(F32))
            matrix = jnp.concatenate(pieces, axis=0)
            out_ref[0, 0, part * TILE : (part + 1) * TILE, :] = matrix.T.astype(BF16)

    return pl.pallas_call(
        body,
        out_shape=jax.ShapeDtypeStruct((slots, plan.range_blocks, PAIR, PAIR), BF16),
        grid=(slots, plan.range_blocks),
        in_specs=[
            pl.BlockSpec((1, 1, TILE), lambda s, j: (s, 0, j)),
            pl.BlockSpec((1, 2, TAPS, TILE), lambda s, j: (s, 0, 0, j)),
        ],
        out_specs=pl.BlockSpec((1, 1, PAIR, PAIR), lambda s, j: (s, j, 0, 0)),
        compiler_params=params(),
        name="build_range",
    )(taps.reshape(slots, 1, -1), weights)


def range_step(plan, starts, matrix, source, target, blocks):
    for j in range(plan.range_blocks):
        rows = pl.ds(aligned(starts(j), TILE), PAIR)
        out = slice(j * TILE, (j + 1) * TILE)
        for block in range(0, blocks, 2):
            count = min(2, blocks - block)
            of_real, of_imag = [
                jnp.dot(
                    matrix(j), source(part, rows, block, count), preferred_element_type=F32
                )
                for part in range(2)
            ]
            real = (of_real[:TILE] - of_imag[TILE:]).astype(BF16)
            imag = (of_real[TILE:] + of_imag[:TILE]).astype(BF16)
            for at in range(count):
                lane = (block + at) * PAIR
                piece = slice(at * TILE, (at + 1) * TILE)
                target[out, lane : lane + TILE] = real[:, piece]
                target[out, lane + TILE : lane + PAIR] = imag[:, piece]


def merge(plan, where, groups, parts, held, rng_blocks, ang_blocks, rng_mats, ang_mats, last_mats):
    half = plan.total_rows // 2
    members = 2
    cells, planes = plan.cells, plan.planes
    width = plan.panel_window
    mwidth = plan.merged_window
    flips = cells - 1
    n_parts = flips * len(groups)
    n_in = n_parts + planes
    flat = [part for per_flip in parts for part in per_flip] + list(held)

    def body(where_ref, rb_ref, ab_ref, *refs):
        ins = refs[:n_in]
        rm_hbm, am_hbm, a2_hbm, own_ref, send_ref = refs[n_in : n_in + 5]
        x_ref, z_ref, y_ref, s_ref, rm_ref, am_ref, a2_ref, sem, wsem = refs[n_in + 5 :]
        panel = where_ref[0]
        side = where_ref[1]
        plane = panel // cells
        cell = lax.rem(panel, cells)
        own_at = plan.panel_start(panel)
        loads = []
        for step in range(planes):
            row = aligned(lax.rem(plane + planes - step, planes) * cells + cell, plan.rows)
            column = own_at - (plan.plane_start(plane) if step else 0)
            loads.append(
                pltpu.make_async_copy(
                    ins[n_parts + step].at[
                        :, :, :, pl.ds(aligned(column, TILE), width * TILE)
                    ],
                    x_ref.at[:, :, pl.ds(row, plan.rows), :],
                    sem.at[step],
                )
            )
        weights = [
            pltpu.make_async_copy(rm_hbm.at[slot], rm_ref.at[slot], wsem.at[slot])
            for slot in range(3)
        ] + [
            pltpu.make_async_copy(am_hbm, am_ref, wsem.at[3]),
            pltpu.make_async_copy(a2_hbm, a2_ref, wsem.at[4]),
        ]
        weights[0].start()
        for load in loads:
            load.start()
        for at in (1, 3, 2, 4):
            weights[at].start()
        for load in loads:
            load.wait()
        for member in range(members):
            for gi, group in enumerate(groups):
                for at, step in enumerate(group):
                    source = lax.rem(plane + planes - step, planes) * cells
                    for flip in range(1, cells):
                        rows = pl.ds(aligned(source + (cell ^ flip), plan.rows), plan.rows)
                        x_ref[member, :, rows, :] = ins[gi * flips + flip - 1][at, member]
            weights[member].wait()
            range_step(
                plan,
                lambda j: rb_ref[member, j],
                lambda j: rm_ref[member, j],
                lambda part, rows, block, count: x_ref[
                    member, part, rows, block * TILE : (block + count) * TILE
                ],
                z_ref.at[member],
                width,
            )
        first = plan.merged_start(panel)
        base = plan.panel_start(panel)
        weights[3].wait()
        for j in range(mwidth):
            terms = []
            for member in range(members):
                start = ab_ref[0, 2 * plan.in_blocks * member + first + j] - base
                terms.append(
                    jnp.dot(
                        z_ref[member, :, pl.ds(aligned(start, PAIR), 2 * PAIR)],
                        am_ref[member * mwidth + j],
                        preferred_element_type=F32,
                    )
                )
            total = (terms[0] + terms[1]).astype(BF16)
            for part in range(2):
                y_ref[part, :, j * TILE : (j + 1) * TILE] = total[
                    :, part * TILE : (part + 1) * TILE
                ]
        weights[2].wait()
        range_step(
            plan,
            lambda j: rb_ref[2, j],
            lambda j: rm_ref[2, j],
            lambda part, rows, block, count: y_ref[
                part, rows, block * TILE : (block + count) * TILE
            ],
            s_ref,
            mwidth,
        )
        weights[4].wait()
        for which, ref in ((1 - side, send_ref), (side, own_ref)):
            for j in range(plan.out_blocks):
                place = 4 * plan.in_blocks + panel * plan.out_blocks + j
                columns = pl.ds(aligned(ab_ref[0, place] - first, PAIR), 2 * PAIR)
                ref[:, j * PAIR : (j + 1) * PAIR] = jnp.dot(
                    s_ref[pl.ds(aligned(which, half), half), columns],
                    a2_ref[j],
                    preferred_element_type=F32,
                ).astype(BF16)

    shape = jax.ShapeDtypeStruct((half, plan.out_blocks * PAIR), BF16)
    rows = plan.total_rows
    return pl.pallas_call(
        body,
        out_shape=[shape, shape],
        in_specs=[SMEM, SMEM, SMEM] + [VMEM] * n_parts + [ANY] * (planes + 3),
        out_specs=[VMEM, VMEM],
        scratch_shapes=[
            pltpu.VMEM((members, 2, rows, width * TILE), BF16),
            pltpu.VMEM((members, rows, width * PAIR), BF16),
            pltpu.VMEM((2, rows, mwidth * TILE), BF16),
            pltpu.VMEM((rows, mwidth * PAIR), BF16),
            pltpu.VMEM(rng_mats.shape, BF16),
            pltpu.VMEM(ang_mats.shape, BF16),
            pltpu.VMEM(last_mats.shape, BF16),
            pltpu.SemaphoreType.DMA((planes,)),
            pltpu.SemaphoreType.DMA((5,)),
        ],
        compiler_params=params(),
        name="merge",
    )(where, rng_blocks, ang_blocks, *flat, rng_mats, ang_mats, last_mats)


def focus(plan, where, own, other, owners, groups):
    half = plan.total_rows // 2
    columns = plan.out_blocks * TILE

    def body(
        where_ref, own_ref, oth_ref, owners_ref, image_ref, grad_ref, held_ref, sem
    ):
        side = where_ref[1]
        row = lax.broadcasted_iota(jnp.int32, (STRIP, TILE), 0) + side * half
        mine, theirs = [], []
        stores = []
        for j in range(plan.out_blocks):
            at = j * PAIR
            sums = [jnp.zeros((8, TILE), F32)] * 2
            for top in range(0, half, STRIP):
                strip = slice(top, top + STRIP)
                weight = 1.0 + 2.0 * (row + top).astype(F32) / (plan.total_rows - 1)
                own_re = own_ref[strip, at : at + TILE].astype(F32)
                own_im = own_ref[strip, at + TILE : at + PAIR].astype(F32)
                oth_re = oth_ref[strip, at : at + TILE].astype(F32)
                oth_im = oth_ref[strip, at + TILE : at + PAIR].astype(F32)
                re = own_re + oth_re
                im = own_im + oth_im
                held_ref[0, strip, j * TILE : (j + 1) * TILE] = re.astype(BF16)
                held_ref[1, strip, j * TILE : (j + 1) * TILE] = im.astype(BF16)
                power = weight * (re * re + im * im)
                for which, (a, b) in enumerate(((own_re, own_im), (oth_re, oth_im))):
                    term = power * (re * a + im * b)
                    sums[which] = sums[which] + jnp.sum(
                        term.reshape(STRIP // 8, 8, TILE), axis=0
                    )
            stores.append(
                pltpu.make_async_copy(
                    held_ref.at[:, :, j * TILE : (j + 1) * TILE],
                    image_ref.at[:, :, j * TILE : (j + 1) * TILE],
                    sem.at[j],
                )
            )
            stores[-1].start()
            mine.append(jnp.sum(sums[0], axis=0, keepdims=True))
            theirs.append(jnp.sum(sums[1], axis=0, keepdims=True))
        mine = jnp.concatenate(mine, axis=1) / plan.total_rows
        theirs = jnp.concatenate(theirs, axis=1) / plan.total_rows
        zeroth = jnp.where(side == 0, mine, theirs)
        oneth = jnp.where(side == 0, theirs, mine)
        marks = owners_ref[...] == lax.broadcasted_iota(
            jnp.int32, (groups, columns), 0
        )
        for q, slope in ((0, zeroth), (1, oneth)):
            grad_ref[q] = jnp.sum(jnp.where(marks, slope, 0.0), axis=1, keepdims=True)
        for store in stores:
            store.wait()

    return pl.pallas_call(
        body,
        out_shape=[
            jax.ShapeDtypeStruct((2, half, columns), BF16),
            jax.ShapeDtypeStruct((2, groups, 1), F32),
        ],
        in_specs=[SMEM, VMEM, VMEM, VMEM],
        out_specs=[ANY, VMEM],
        scratch_shapes=[
            pltpu.VMEM((2, half, columns), BF16),
            pltpu.SemaphoreType.DMA((plan.out_blocks,)),
        ],
        compiler_params=params(),
        name="focus",
    )(where, own, other, owners)


def shards(subimages, rng_taps, rng_blocks, rng_weights, ang_taps, ang_blocks, ang_weights, owners):
    panels = lax.axis_size("panel")
    panel = lax.axis_index("panel").astype(jnp.int32)
    side = lax.axis_index("aper").astype(jnp.int32)
    groups = GRP_DEV * panels
    plan = Plan(panels, subimages.shape[2], subimages.shape[3])
    where = jnp.stack([panel, side])

    def plane_shift(step):
        return [
            (g * plan.cells + c, ((g + step) % plan.planes) * plan.cells + c)
            for g in range(plan.planes)
            for c in range(plan.cells)
        ]

    def cell_flip(flip):
        return [(i, i ^ flip) for i in range(panels)]

    steps = [
        sorted({step, plan.planes - step}) for step in range(1, plan.planes // 2 + 1)
    ]
    order = [[0]] + steps
    rest = [step for group in steps[1:] for step in group]
    soon, _ = pack_own(plan, where, subimages, steps[0], [])
    later, near_parts = pack_own(plan, where, subimages, rest, range(1, plan.cells))
    far = dict(zip(steps[0] + rest, list(soon) + list(later)))

    def across(pieces):
        return [
            lax.ppermute(pieces[flip - 1], "panel", cell_flip(flip))
            for flip in range(1, plan.cells)
        ]

    parts = []
    held = {0: subimages}
    packed = near_parts
    arrived = {
        step: lax.ppermute(far[step], "panel", plane_shift(step))
        for group in steps
        for step in group
    }
    for group in steps:
        received = [arrived[step] for step in group]
        parts.append(across(packed))
        tied = [parts[-1][0]] if len(parts) > 1 else parts[-1]
        tied, received = lax.optimization_barrier((tied, received))
        parts[-1][: len(tied)] = tied
        held.update(zip(group, received))
        packed = pack_panels(plan, where, received)
    parts.append(across(packed))
    held = [held[step] for step in range(plan.planes)]

    first = plan.merged_start(panel)
    near = first + jnp.arange(plan.merged_window, dtype=jnp.int32)
    merge_at = jnp.concatenate([near, 2 * plan.in_blocks + near])
    last_at = (
        4 * plan.in_blocks
        + panel * plan.out_blocks
        + jnp.arange(plan.out_blocks, dtype=jnp.int32)
    )
    ang_mats = build_angle(merge_at, ang_taps, ang_weights[0])
    last_mats = build_angle(last_at, ang_taps, ang_weights[0])
    rng_mats = build_range(plan, rng_taps[0], rng_weights[0])

    own, send = merge(
        plan, where, order, parts, held, rng_blocks[0], ang_blocks, rng_mats, ang_mats, last_mats
    )
    other = lax.ppermute(send, "aper", [(0, 1), (1, 0)])
    columns = plan.out_blocks * TILE
    mine = lax.dynamic_slice_in_dim(owners[None], panel * columns, columns, 1)
    image, partials = focus(plan, where, own, other, mine, groups)
    pieces = lax.all_to_all(
        partials.reshape(2 * panels, GRP_DEV), ("aper", "panel"), 0, 0, tiled=True
    )
    return image, jnp.sum(pieces, axis=0)[None]


def solution(mesh):
    return jax.shard_map(
        shards,
        mesh=mesh,
        in_specs=(
            P(("scene", "aper"), None, "panel", None),
            P("aper", None, None),
            P("aper", None, None),
            P("aper", None, None, None, None),
            P("aper", None),
            P("aper", None),
            P("aper", None, None, None),
            P(),
        ),
        out_specs=(P(None, ("scene", "aper"), "panel"), P(("scene", "aper"), "panel")),
        check_vma=False,
    )
```

```python
import jax
import jax.numpy as jnp
from jax import lax
from jax.experimental import pallas as pl
from jax.experimental.pallas import tpu as pltpu
from jax.sharding import PartitionSpec as P

TILE = 128
PAIR = 2 * TILE
TAPS = 16
GRP_DEV = 4
STRIP = 32
F32 = jnp.float32
BF16 = jnp.bfloat16
VMEM_BYTES = 44 * 1024 * 1024


def aligned(value, step):
    return pl.multiple_of(value * step, step)


def params():
    return pltpu.CompilerParams(vmem_limit_bytes=VMEM_BYTES)


class Plan:
    def __init__(self, panels, rows, angles):
        self.panels = panels
        self.rows = rows
        self.total_rows = rows * panels
        self.in_blocks = angles // TILE
        self.own = self.in_blocks // panels
        self.cells = TILE // rows
        self.planes = panels // self.cells
        self.range_blocks = self.total_rows // TILE
        self.plane_window = min(self.cells * self.own + 4, self.in_blocks)
        self.panel_window = self.own + 4
        self.merged_window = 2 * self.own + 2
        self.out_blocks = 4 * self.own

    def plane_start(self, plane):
        return jnp.clip(
            self.cells * self.own * plane - 2, 0, self.in_blocks - self.plane_window
        )

    def panel_start(self, panel):
        return jnp.clip(self.own * panel - 2, 0, self.in_blocks - self.panel_window)

    def merged_start(self, panel):
        return jnp.clip(
            2 * self.own * panel - 1, 0, 2 * self.in_blocks - self.merged_window
        )


SMEM = pl.BlockSpec(memory_space=pltpu.SMEM)
VMEM = pl.BlockSpec(memory_space=pltpu.VMEM)
ANY = pl.BlockSpec(memory_space=pl.ANY)


def pack_own(plan, where, subimages, steps, flips):
    members = subimages.shape[0]
    others = len(steps)

    def body(where_ref, x_ref, *outs):
        panel = where_ref[0]
        plane = panel // plan.cells
        cell = lax.rem(panel, plan.cells)
        for at, step in enumerate(steps):
            target = lax.rem(plane + step, plan.planes)
            column = aligned(plan.plane_start(target), TILE)
            outs[at][...] = x_ref[:, :, :, pl.ds(column, plan.plane_window * TILE)]
        for at, flip in enumerate(flips):
            target = plane * plan.cells + (cell ^ flip)
            column = aligned(plan.panel_start(target), TILE)
            outs[others + at][0] = x_ref[:, :, :, pl.ds(column, plan.panel_window * TILE)]

    lead = (members, 2, plan.rows)
    far = jax.ShapeDtypeStruct(lead + (plan.plane_window * TILE,), BF16)
    near = jax.ShapeDtypeStruct((1,) + lead + (plan.panel_window * TILE,), BF16)
    outs = pl.pallas_call(
        body,
        out_shape=[far] * others + [near] * len(flips),
        in_specs=[SMEM, VMEM],
        out_specs=[VMEM] * (others + len(flips)),
        compiler_params=params(),
        name="pack_own",
    )(where, subimages)
    return outs[:others], outs[others:]


def pack_panels(plan, where, received):
    count = len(received)

    def body(where_ref, *refs):
        ins, outs = refs[:count], refs[count:]
        panel = where_ref[0]
        plane = panel // plan.cells
        cell = lax.rem(panel, plan.cells)
        base = plan.plane_start(plane)
        for flip in range(1, plan.cells):
            offset = plan.panel_start(plane * plan.cells + (cell ^ flip)) - base
            columns = pl.ds(aligned(offset, TILE), plan.panel_window * TILE)
            for at in range(count):
                outs[flip - 1][at] = ins[at][:, :, :, columns]

    lead = received[0].shape[:3]
    shape = jax.ShapeDtypeStruct(
        (count,) + lead + (plan.panel_window * TILE,), BF16
    )
    return pl.pallas_call(
        body,
        out_shape=[shape] * (plan.cells - 1),
        in_specs=[SMEM] + [VMEM] * count,
        out_specs=[VMEM] * (plan.cells - 1),
        compiler_params=params(),
        name="pack_panels",
    )(where, *received)


def spread_taps(base, weights):
    low = base & (TAPS - 1)
    high = base >> 4
    wide = jnp.concatenate([weights, jnp.zeros_like(weights)], axis=0)
    for bit in range(4):
        moved = pltpu.roll(wide, 1 << bit, axis=0)
        wide = jnp.where(((low >> bit) & 1) == 1, moved, wide)
    zero = jnp.zeros_like(weights)
    pieces = []
    for place in range(PAIR // TAPS):
        below = jnp.where(high == place - 1, wide[TAPS:], zero)
        pieces.append(jnp.where(high == place, wide[:TAPS], below))
    return pieces


def build_angle(blocks, taps, weights):
    count = blocks.shape[0]

    def body(blocks_ref, taps_ref, weights_ref, out_ref):
        base = taps_ref[...]
        real = spread_taps(base, weights_ref[0].astype(F32))
        imag = spread_taps(base, weights_ref[1].astype(F32))
        half = TILE // TAPS
        for place in range(PAIR // TAPS):
            row = (place // half) * PAIR + (place % half) * TAPS
            re = real[place].astype(BF16)
            im = imag[place].astype(BF16)
            neg = (-imag[place]).astype(BF16)
            out_ref[0, row : row + TAPS, :TILE] = re
            out_ref[0, row : row + TAPS, TILE:] = im
            out_ref[0, TILE + row : TILE + row + TAPS, :TILE] = neg
            out_ref[0, TILE + row : TILE + row + TAPS, TILE:] = re

    return pl.pallas_call(
        body,
        out_shape=jax.ShapeDtypeStruct((count, 2 * PAIR, PAIR), BF16),
        grid_spec=pltpu.PrefetchScalarGridSpec(
            num_scalar_prefetch=1,
            grid=(count,),
            in_specs=[
                pl.BlockSpec((1, TILE), lambda i, t: (0, t[i])),
                pl.BlockSpec((2, TAPS, TILE), lambda i, t: (0, 0, t[i])),
            ],
            out_specs=pl.BlockSpec((1, 2 * PAIR, PAIR), lambda i, t: (i, 0, 0)),
        ),
        compiler_params=params(),
        name="build_angle",
    )(blocks, taps, weights)


def build_range(plan, taps, weights):
    slots = taps.shape[0]

    def body(taps_ref, weights_ref, out_ref):
        base = taps_ref[0]
        for part in range(2):
            pieces = spread_taps(base, weights_ref[0, part].astype(F32))
            matrix = jnp.concatenate(pieces, axis=0)
            out_ref[0, 0, part * TILE : (part + 1) * TILE, :] = matrix.T.astype(BF16)

    return pl.pallas_call(
        body,
        out_shape=jax.ShapeDtypeStruct((slots, plan.range_blocks, PAIR, PAIR), BF16),
        grid=(slots, plan.range_blocks),
        in_specs=[
            pl.BlockSpec((1, 1, TILE), lambda s, j: (s, 0, j)),
            pl.BlockSpec((1, 2, TAPS, TILE), lambda s, j: (s, 0, 0, j)),
        ],
        out_specs=pl.BlockSpec((1, 1, PAIR, PAIR), lambda s, j: (s, j, 0, 0)),
        compiler_params=params(),
        name="build_range",
    )(taps.reshape(slots, 1, -1), weights)


def range_step(plan, starts, matrix, source, target, blocks):
    for j in range(plan.range_blocks):
        rows = pl.ds(aligned(starts(j), TILE), PAIR)
        out = slice(j * TILE, (j + 1) * TILE)
        for block in range(0, blocks, 2):
            count = min(2, blocks - block)
            of_real, of_imag = [
                jnp.dot(
                    matrix(j), source(part, rows, block, count), preferred_element_type=F32
                )
                for part in range(2)
            ]
            real = (of_real[:TILE] - of_imag[TILE:]).astype(BF16)
            imag = (of_real[TILE:] + of_imag[:TILE]).astype(BF16)
            for at in range(count):
                lane = (block + at) * PAIR
                piece = slice(at * TILE, (at + 1) * TILE)
                target[out, lane : lane + TILE] = real[:, piece]
                target[out, lane + TILE : lane + PAIR] = imag[:, piece]


def merge(plan, where, groups, parts, held, rng_blocks, ang_blocks, rng_mats, ang_mats, last_mats):
    half = plan.total_rows // 2
    members = 2
    cells, planes = plan.cells, plan.planes
    width = plan.panel_window
    mwidth = plan.merged_window
    flips = cells - 1
    n_parts = flips * len(groups)
    n_in = n_parts + planes
    flat = [part for per_flip in parts for part in per_flip] + list(held)

    def body(where_ref, rb_ref, ab_ref, *refs):
        ins = refs[:n_in]
        rm_hbm, am_hbm, a2_hbm, own_ref, send_ref = refs[n_in : n_in + 5]
        x_ref, z_ref, y_ref, s_ref, rm_ref, am_ref, a2_ref, sem, wsem, o_ref, osem = refs[n_in + 5 :]
        panel = where_ref[0]
        side = where_ref[1]
        plane = panel // cells
        cell = lax.rem(panel, cells)
        own_at = plan.panel_start(panel)
        loads = []
        for step in range(planes):
            row = aligned(lax.rem(plane + planes - step, planes) * cells + cell, plan.rows)
            column = own_at - (plan.plane_start(plane) if step else 0)
            loads.append(
                pltpu.make_async_copy(
                    ins[n_parts + step].at[
                        :, :, :, pl.ds(aligned(column, TILE), width * TILE)
                    ],
                    x_ref.at[:, :, pl.ds(row, plan.rows), :],
                    sem.at[step],
                )
            )
        weights = [
            pltpu.make_async_copy(rm_hbm.at[slot], rm_ref.at[slot], wsem.at[slot])
            for slot in range(3)
        ] + [
            pltpu.make_async_copy(am_hbm, am_ref, wsem.at[3]),
            pltpu.make_async_copy(a2_hbm, a2_ref, wsem.at[4]),
        ]
        weights[0].start()
        for load in loads:
            load.start()
        for at in (1, 3, 2, 4):
            weights[at].start()
        for member in range(members):
            for gi, group in enumerate(groups):
                for at, step in enumerate(group):
                    source = lax.rem(plane + planes - step, planes) * cells
                    for flip in range(1, cells):
                        rows = pl.ds(aligned(source + (cell ^ flip), plan.rows), plan.rows)
                        x_ref[member, :, rows, :] = ins[gi * flips + flip - 1][at, member]
            if member == 0:
                for load in loads:
                    load.wait()
            weights[member].wait()
            range_step(
                plan,
                lambda j: rb_ref[member, j],
                lambda j: rm_ref[member, j],
                lambda part, rows, block, count: x_ref[
                    member, part, rows, block * TILE : (block + count) * TILE
                ],
                z_ref.at[member],
                width,
            )
        first = plan.merged_start(panel)
        base = plan.panel_start(panel)
        weights[3].wait()
        for j in range(mwidth):
            terms = []
            for member in range(members):
                start = ab_ref[0, 2 * plan.in_blocks * member + first + j] - base
                terms.append(
                    jnp.dot(
                        z_ref[member, :, pl.ds(aligned(start, PAIR), 2 * PAIR)],
                        am_ref[member * mwidth + j],
                        preferred_element_type=F32,
                    )
                )
            total = (terms[0] + terms[1]).astype(BF16)
            for part in range(2):
                y_ref[part, :, j * TILE : (j + 1) * TILE] = total[
                    :, part * TILE : (part + 1) * TILE
                ]
        weights[2].wait()
        range_step(
            plan,
            lambda j: rb_ref[2, j],
            lambda j: rm_ref[2, j],
            lambda part, rows, block, count: y_ref[
                part, rows, block * TILE : (block + count) * TILE
            ],
            s_ref,
            mwidth,
        )
        weights[4].wait()
        stores = []
        for turn, (which, ref) in enumerate(((1 - side, send_ref), (side, own_ref))):
            for j in range(plan.out_blocks):
                place = 4 * plan.in_blocks + panel * plan.out_blocks + j
                columns = pl.ds(aligned(ab_ref[0, place] - first, PAIR), 2 * PAIR)
                out = slice(j * PAIR, (j + 1) * PAIR)
                o_ref[turn, :, out] = jnp.dot(
                    s_ref[pl.ds(aligned(which, half), half), columns],
                    a2_ref[j],
                    preferred_element_type=F32,
                ).astype(BF16)
                if j % 4 == 3:
                    four = slice((j - 3) * PAIR, (j + 1) * PAIR)
                    stores.append(
                        pltpu.make_async_copy(
                            o_ref.at[turn, :, four], ref.at[:, four], osem.at[len(stores)]
                        )
                    )
                    stores[-1].start()
        for store in stores:
            store.wait()

    shape = jax.ShapeDtypeStruct((half, plan.out_blocks * PAIR), BF16)
    rows = plan.total_rows
    return pl.pallas_call(
        body,
        out_shape=[shape, shape],
        in_specs=[SMEM, SMEM, SMEM] + [VMEM] * n_parts + [ANY] * (planes + 3),
        out_specs=[ANY, ANY],
        scratch_shapes=[
            pltpu.VMEM((members, 2, rows, width * TILE), BF16),
            pltpu.VMEM((members, rows, width * PAIR), BF16),
            pltpu.VMEM((2, rows, mwidth * TILE), BF16),
            pltpu.VMEM((rows, mwidth * PAIR), BF16),
            pltpu.VMEM(rng_mats.shape, BF16),
            pltpu.VMEM(ang_mats.shape, BF16),
            pltpu.VMEM(last_mats.shape, BF16),
            pltpu.SemaphoreType.DMA((planes,)),
            pltpu.SemaphoreType.DMA((5,)),
            pltpu.VMEM((2,) + shape.shape, BF16),
            pltpu.SemaphoreType.DMA((plan.out_blocks // 2,)),
        ],
        compiler_params=params(),
        name="merge",
    )(where, rng_blocks, ang_blocks, *flat, rng_mats, ang_mats, last_mats)


def focus(plan, where, own, other, owners, groups):
    half = plan.total_rows // 2
    columns = plan.out_blocks * TILE

    def body(
        where_ref, own_ref, oth_ref, owners_ref, image_ref, grad_ref, held_ref, sem
    ):
        side = where_ref[1]
        row = lax.broadcasted_iota(jnp.int32, (STRIP, TILE), 0) + side * half
        mine, theirs = [], []
        stores = []
        for j in range(plan.out_blocks):
            at = j * PAIR
            sums = [jnp.zeros((8, TILE), F32)] * 2
            for top in range(0, half, STRIP):
                strip = slice(top, top + STRIP)
                weight = 1.0 + 2.0 * (row + top).astype(F32) / (plan.total_rows - 1)
                own_re = own_ref[strip, at : at + TILE].astype(F32)
                own_im = own_ref[strip, at + TILE : at + PAIR].astype(F32)
                oth_re = oth_ref[strip, at : at + TILE].astype(F32)
                oth_im = oth_ref[strip, at + TILE : at + PAIR].astype(F32)
                re = own_re + oth_re
                im = own_im + oth_im
                held_ref[0, strip, j * TILE : (j + 1) * TILE] = re.astype(BF16)
                held_ref[1, strip, j * TILE : (j + 1) * TILE] = im.astype(BF16)
                power = weight * (re * re + im * im)
                for which, (a, b) in enumerate(((own_re, own_im), (oth_re, oth_im))):
                    term = power * (re * a + im * b)
                    sums[which] = sums[which] + jnp.sum(
                        term.reshape(STRIP // 8, 8, TILE), axis=0
                    )
            stores.append(
                pltpu.make_async_copy(
                    held_ref.at[:, :, j * TILE : (j + 1) * TILE],
                    image_ref.at[:, :, j * TILE : (j + 1) * TILE],
                    sem.at[j],
                )
            )
            stores[-1].start()
            mine.append(jnp.sum(sums[0], axis=0, keepdims=True))
            theirs.append(jnp.sum(sums[1], axis=0, keepdims=True))
        mine = jnp.concatenate(mine, axis=1) / plan.total_rows
        theirs = jnp.concatenate(theirs, axis=1) / plan.total_rows
        zeroth = jnp.where(side == 0, mine, theirs)
        oneth = jnp.where(side == 0, theirs, mine)
        marks = owners_ref[...] == lax.broadcasted_iota(
            jnp.int32, (groups, columns), 0
        )
        for q, slope in ((0, zeroth), (1, oneth)):
            grad_ref[q] = jnp.sum(jnp.where(marks, slope, 0.0), axis=1, keepdims=True)
        for store in stores:
            store.wait()

    return pl.pallas_call(
        body,
        out_shape=[
            jax.ShapeDtypeStruct((2, half, columns), BF16),
            jax.ShapeDtypeStruct((2, groups, 1), F32),
        ],
        in_specs=[SMEM, VMEM, VMEM, VMEM],
        out_specs=[ANY, VMEM],
        scratch_shapes=[
            pltpu.VMEM((2, half, columns), BF16),
            pltpu.SemaphoreType.DMA((plan.out_blocks,)),
        ],
        compiler_params=params(),
        name="focus",
    )(where, own, other, owners)


def shards(subimages, rng_taps, rng_blocks, rng_weights, ang_taps, ang_blocks, ang_weights, owners):
    panels = lax.axis_size("panel")
    panel = lax.axis_index("panel").astype(jnp.int32)
    side = lax.axis_index("aper").astype(jnp.int32)
    groups = GRP_DEV * panels
    plan = Plan(panels, subimages.shape[2], subimages.shape[3])
    where = jnp.stack([panel, side])

    def plane_shift(step):
        return [
            (g * plan.cells + c, ((g + step) % plan.planes) * plan.cells + c)
            for g in range(plan.planes)
            for c in range(plan.cells)
        ]

    def cell_flip(flip):
        return [(i, i ^ flip) for i in range(panels)]

    steps = [
        sorted({step, plan.planes - step}) for step in range(1, plan.planes // 2 + 1)
    ]
    order = [[0]] + steps
    rest = [step for group in steps[1:] for step in group]
    soon, _ = pack_own(plan, where, subimages, steps[0], [])
    later, near_parts = pack_own(plan, where, subimages, rest, range(1, plan.cells))
    far = dict(zip(steps[0] + rest, list(soon) + list(later)))

    def across(pieces):
        return [
            lax.ppermute(pieces[flip - 1], "panel", cell_flip(flip))
            for flip in range(1, plan.cells)
        ]

    parts = []
    held = {0: subimages}
    packed = near_parts
    arrived = {
        step: lax.ppermute(far[step], "panel", plane_shift(step))
        for group in steps
        for step in group
    }
    for group in steps:
        received = [arrived[step] for step in group]
        parts.append(across(packed))
        tied = [parts[-1][0]] if len(parts) > 1 else parts[-1]
        tied, received = lax.optimization_barrier((tied, received))
        parts[-1][: len(tied)] = tied
        held.update(zip(group, received))
        packed = pack_panels(plan, where, received)
    parts.append(across(packed))
    held = [held[step] for step in range(plan.planes)]

    first = plan.merged_start(panel)
    near = first + jnp.arange(plan.merged_window, dtype=jnp.int32)
    merge_at = jnp.concatenate([near, 2 * plan.in_blocks + near])
    last_at = (
        4 * plan.in_blocks
        + panel * plan.out_blocks
        + jnp.arange(plan.out_blocks, dtype=jnp.int32)
    )
    ang_mats = build_angle(merge_at, ang_taps, ang_weights[0])
    last_mats = build_angle(last_at, ang_taps, ang_weights[0])
    rng_mats = build_range(plan, rng_taps[0], rng_weights[0])

    own, send = merge(
        plan, where, order, parts, held, rng_blocks[0], ang_blocks, rng_mats, ang_mats, last_mats
    )
    other = lax.ppermute(send, "aper", [(0, 1), (1, 0)])
    columns = plan.out_blocks * TILE
    mine = lax.dynamic_slice_in_dim(owners[None], panel * columns, columns, 1)
    image, partials = focus(plan, where, own, other, mine, groups)
    pieces = lax.all_to_all(
        partials.reshape(2 * panels, GRP_DEV), ("aper", "panel"), 0, 0, tiled=True
    )
    return image, jnp.sum(pieces, axis=0)[None]


def solution(mesh):
    return jax.shard_map(
        shards,
        mesh=mesh,
        in_specs=(
            P(("scene", "aper"), None, "panel", None),
            P("aper", None, None),
            P("aper", None, None),
            P("aper", None, None, None, None),
            P("aper", None),
            P("aper", None),
            P("aper", None, None, None),
            P(),
        ),
        out_specs=(P(None, ("scene", "aper"), "panel"), P(("scene", "aper"), "panel")),
        check_vma=False,
    )
```

```python
import jax
import jax.numpy as jnp
from jax import lax
from jax.experimental import pallas as pl
from jax.experimental.pallas import tpu as pltpu
from jax.sharding import PartitionSpec as P

TILE = 128
PAIR = 2 * TILE
TAPS = 16
GRP_DEV = 4
STRIP = 32
F32 = jnp.float32
BF16 = jnp.bfloat16
VMEM_BYTES = 44 * 1024 * 1024


def aligned(value, step):
    return pl.multiple_of(value * step, step)


def params():
    return pltpu.CompilerParams(vmem_limit_bytes=VMEM_BYTES)


class Plan:
    def __init__(self, panels, rows, angles):
        self.panels = panels
        self.rows = rows
        self.total_rows = rows * panels
        self.in_blocks = angles // TILE
        self.own = self.in_blocks // panels
        self.cells = TILE // rows
        self.planes = panels // self.cells
        self.range_blocks = self.total_rows // TILE
        self.plane_window = min(self.cells * self.own + 4, self.in_blocks)
        self.panel_window = self.own + 4
        self.merged_window = 2 * self.own + 2
        self.out_blocks = 4 * self.own

    def plane_start(self, plane):
        return jnp.clip(
            self.cells * self.own * plane - 2, 0, self.in_blocks - self.plane_window
        )

    def panel_start(self, panel):
        return jnp.clip(self.own * panel - 2, 0, self.in_blocks - self.panel_window)

    def merged_start(self, panel):
        return jnp.clip(
            2 * self.own * panel - 1, 0, 2 * self.in_blocks - self.merged_window
        )


SMEM = pl.BlockSpec(memory_space=pltpu.SMEM)
VMEM = pl.BlockSpec(memory_space=pltpu.VMEM)
ANY = pl.BlockSpec(memory_space=pl.ANY)


def pack_own(plan, where, subimages, steps, flips):
    members = subimages.shape[0]
    others = len(steps)

    def body(where_ref, x_ref, *outs):
        panel = where_ref[0]
        plane = panel // plan.cells
        cell = lax.rem(panel, plan.cells)
        for at, step in enumerate(steps):
            target = lax.rem(plane + step, plan.planes)
            column = aligned(plan.plane_start(target), TILE)
            outs[at][...] = x_ref[:, :, :, pl.ds(column, plan.plane_window * TILE)]
        for at, flip in enumerate(flips):
            target = plane * plan.cells + (cell ^ flip)
            column = aligned(plan.panel_start(target), TILE)
            outs[others + at][0] = x_ref[:, :, :, pl.ds(column, plan.panel_window * TILE)]

    lead = (members, 2, plan.rows)
    far = jax.ShapeDtypeStruct(lead + (plan.plane_window * TILE,), BF16)
    near = jax.ShapeDtypeStruct((1,) + lead + (plan.panel_window * TILE,), BF16)
    outs = pl.pallas_call(
        body,
        out_shape=[far] * others + [near] * len(flips),
        in_specs=[SMEM, VMEM],
        out_specs=[VMEM] * (others + len(flips)),
        compiler_params=params(),
        name="pack_own",
    )(where, subimages)
    return outs[:others], outs[others:]


def pack_panels(plan, where, received):
    count = len(received)

    def body(where_ref, *refs):
        ins, outs = refs[:count], refs[count:]
        panel = where_ref[0]
        plane = panel // plan.cells
        cell = lax.rem(panel, plan.cells)
        base = plan.plane_start(plane)
        for flip in range(1, plan.cells):
            offset = plan.panel_start(plane * plan.cells + (cell ^ flip)) - base
            columns = pl.ds(aligned(offset, TILE), plan.panel_window * TILE)
            for at in range(count):
                outs[flip - 1][at] = ins[at][:, :, :, columns]

    lead = received[0].shape[:3]
    shape = jax.ShapeDtypeStruct(
        (count,) + lead + (plan.panel_window * TILE,), BF16
    )
    return pl.pallas_call(
        body,
        out_shape=[shape] * (plan.cells - 1),
        in_specs=[SMEM] + [VMEM] * count,
        out_specs=[VMEM] * (plan.cells - 1),
        compiler_params=params(),
        name="pack_panels",
    )(where, *received)


def spread_taps(base, weights):
    low = base & (TAPS - 1)
    high = base >> 4
    wide = jnp.concatenate([weights, jnp.zeros_like(weights)], axis=0)
    for bit in range(4):
        moved = pltpu.roll(wide, 1 << bit, axis=0)
        wide = jnp.where(((low >> bit) & 1) == 1, moved, wide)
    zero = jnp.zeros_like(weights)
    pieces = []
    for place in range(PAIR // TAPS):
        below = jnp.where(high == place - 1, wide[TAPS:], zero)
        pieces.append(jnp.where(high == place, wide[:TAPS], below))
    return pieces


def build_angle(blocks, taps, weights):
    count = blocks.shape[0]

    def body(blocks_ref, taps_ref, weights_ref, out_ref):
        base = taps_ref[...]
        real = spread_taps(base, weights_ref[0].astype(F32))
        imag = spread_taps(base, weights_ref[1].astype(F32))
        half = TILE // TAPS
        for place in range(PAIR // TAPS):
            row = (place // half) * PAIR + (place % half) * TAPS
            re = real[place].astype(BF16)
            im = imag[place].astype(BF16)
            neg = (-imag[place]).astype(BF16)
            out_ref[0, row : row + TAPS, :TILE] = re
            out_ref[0, row : row + TAPS, TILE:] = im
            out_ref[0, TILE + row : TILE + row + TAPS, :TILE] = neg
            out_ref[0, TILE + row : TILE + row + TAPS, TILE:] = re

    return pl.pallas_call(
        body,
        out_shape=jax.ShapeDtypeStruct((count, 2 * PAIR, PAIR), BF16),
        grid_spec=pltpu.PrefetchScalarGridSpec(
            num_scalar_prefetch=1,
            grid=(count,),
            in_specs=[
                pl.BlockSpec((1, TILE), lambda i, t: (0, t[i])),
                pl.BlockSpec((2, TAPS, TILE), lambda i, t: (0, 0, t[i])),
            ],
            out_specs=pl.BlockSpec((1, 2 * PAIR, PAIR), lambda i, t: (i, 0, 0)),
        ),
        compiler_params=params(),
        name="build_angle",
    )(blocks, taps, weights)


def build_range(plan, taps, weights):
    slots = taps.shape[0]

    def body(taps_ref, weights_ref, out_ref):
        base = taps_ref[0]
        for part in range(2):
            pieces = spread_taps(base, weights_ref[0, part].astype(F32))
            matrix = jnp.concatenate(pieces, axis=0)
            out_ref[0, 0, part * TILE : (part + 1) * TILE, :] = matrix.T.astype(BF16)

    return pl.pallas_call(
        body,
        out_shape=jax.ShapeDtypeStruct((slots, plan.range_blocks, PAIR, PAIR), BF16),
        grid=(slots, plan.range_blocks),
        in_specs=[
            pl.BlockSpec((1, 1, TILE), lambda s, j: (s, 0, j)),
            pl.BlockSpec((1, 2, TAPS, TILE), lambda s, j: (s, 0, 0, j)),
        ],
        out_specs=pl.BlockSpec((1, 1, PAIR, PAIR), lambda s, j: (s, j, 0, 0)),
        compiler_params=params(),
        name="build_range",
    )(taps.reshape(slots, 1, -1), weights)


def range_step(plan, starts, matrix, source, target, blocks):
    for j in range(plan.range_blocks):
        rows = pl.ds(aligned(starts(j), TILE), PAIR)
        out = slice(j * TILE, (j + 1) * TILE)
        for block in range(0, blocks, 2):
            count = min(2, blocks - block)
            of_real, of_imag = [
                jnp.dot(
                    matrix(j), source(part, rows, block, count), preferred_element_type=F32
                )
                for part in range(2)
            ]
            real = (of_real[:TILE] - of_imag[TILE:]).astype(BF16)
            imag = (of_real[TILE:] + of_imag[:TILE]).astype(BF16)
            for at in range(count):
                lane = (block + at) * PAIR
                piece = slice(at * TILE, (at + 1) * TILE)
                target[out, lane : lane + TILE] = real[:, piece]
                target[out, lane + TILE : lane + PAIR] = imag[:, piece]


def merge(plan, where, groups, parts, held, rng_blocks, ang_blocks, rng_mats, ang_mats, last_mats):
    half = plan.total_rows // 2
    members = 2
    cells, planes = plan.cells, plan.planes
    width = plan.panel_window
    mwidth = plan.merged_window
    flips = cells - 1
    n_parts = flips * len(groups)
    n_in = n_parts + planes
    flat = [part for per_flip in parts for part in per_flip] + list(held)

    def body(where_ref, rb_ref, ab_ref, *refs):
        ins = refs[:n_in]
        rm_hbm, am_hbm, a2_hbm, own_ref, send_ref = refs[n_in : n_in + 5]
        x_ref, z_ref, y_ref, s_ref, rm_ref, am_ref, a2_ref, sem, wsem, o_ref, osem = refs[n_in + 5 :]
        panel = where_ref[0]
        side = where_ref[1]
        plane = panel // cells
        cell = lax.rem(panel, cells)
        own_at = plan.panel_start(panel)
        loads = []
        for step in range(planes):
            row = aligned(lax.rem(plane + planes - step, planes) * cells + cell, plan.rows)
            column = own_at - (plan.plane_start(plane) if step else 0)
            loads.append(
                pltpu.make_async_copy(
                    ins[n_parts + step].at[
                        :, :, :, pl.ds(aligned(column, TILE), width * TILE)
                    ],
                    x_ref.at[:, :, pl.ds(row, plan.rows), :],
                    sem.at[step],
                )
            )
        weights = [
            pltpu.make_async_copy(rm_hbm.at[slot], rm_ref.at[slot], wsem.at[slot])
            for slot in range(3)
        ] + [
            pltpu.make_async_copy(am_hbm, am_ref, wsem.at[3]),
            pltpu.make_async_copy(a2_hbm, a2_ref, wsem.at[4]),
        ]
        weights[0].start()
        for load in loads:
            load.start()
        for at in (1, 3, 2, 4):
            weights[at].start()
        for member in range(members):
            for gi, group in enumerate(groups):
                for at, step in enumerate(group):
                    source = lax.rem(plane + planes - step, planes) * cells
                    for flip in range(1, cells):
                        rows = pl.ds(aligned(source + (cell ^ flip), plan.rows), plan.rows)
                        x_ref[member, :, rows, :] = ins[gi * flips + flip - 1][at, member]
            if member == 0:
                for load in loads:
                    load.wait()
            weights[member].wait()
            range_step(
                plan,
                lambda j: rb_ref[member, j],
                lambda j: rm_ref[member, j],
                lambda part, rows, block, count: x_ref[
                    member, part, rows, block * TILE : (block + count) * TILE
                ],
                z_ref.at[member],
                width,
            )
        first = plan.merged_start(panel)
        base = plan.panel_start(panel)
        weights[3].wait()
        for j in range(mwidth):
            terms = []
            for member in range(members):
                start = ab_ref[0, 2 * plan.in_blocks * member + first + j] - base
                terms.append(
                    jnp.dot(
                        z_ref[member, :, pl.ds(aligned(start, PAIR), 2 * PAIR)],
                        am_ref[member * mwidth + j],
                        preferred_element_type=F32,
                    )
                )
            total = (terms[0] + terms[1]).astype(BF16)
            for part in range(2):
                y_ref[part, :, j * TILE : (j + 1) * TILE] = total[
                    :, part * TILE : (part + 1) * TILE
                ]
        weights[2].wait()
        range_step(
            plan,
            lambda j: rb_ref[2, j],
            lambda j: rm_ref[2, j],
            lambda part, rows, block, count: y_ref[
                part, rows, block * TILE : (block + count) * TILE
            ],
            s_ref,
            mwidth,
        )
        weights[4].wait()
        stores = []
        for turn, (which, ref) in enumerate(((1 - side, send_ref), (side, own_ref))):
            for j in range(plan.out_blocks):
                place = 4 * plan.in_blocks + panel * plan.out_blocks + j
                columns = pl.ds(aligned(ab_ref[0, place] - first, PAIR), 2 * PAIR)
                out = slice(j * PAIR, (j + 1) * PAIR)
                o_ref[turn, :, out] = jnp.dot(
                    s_ref[pl.ds(aligned(which, half), half), columns],
                    a2_ref[j],
                    preferred_element_type=F32,
                ).astype(BF16)
                if j % 4 == 3:
                    four = slice((j - 3) * PAIR, (j + 1) * PAIR)
                    stores.append(
                        pltpu.make_async_copy(
                            o_ref.at[turn, :, four], ref.at[:, four], osem.at[len(stores)]
                        )
                    )
                    stores[-1].start()
        for store in stores:
            store.wait()

    shape = jax.ShapeDtypeStruct((half, plan.out_blocks * PAIR), BF16)
    rows = plan.total_rows
    return pl.pallas_call(
        body,
        out_shape=[shape, shape],
        in_specs=[SMEM, SMEM, SMEM] + [VMEM] * n_parts + [ANY] * (planes + 3),
        out_specs=[ANY, ANY],
        scratch_shapes=[
            pltpu.VMEM((members, 2, rows, width * TILE), BF16),
            pltpu.VMEM((members, rows, width * PAIR), BF16),
            pltpu.VMEM((2, rows, mwidth * TILE), BF16),
            pltpu.VMEM((rows, mwidth * PAIR), BF16),
            pltpu.VMEM(rng_mats.shape, BF16),
            pltpu.VMEM(ang_mats.shape, BF16),
            pltpu.VMEM(last_mats.shape, BF16),
            pltpu.SemaphoreType.DMA((planes,)),
            pltpu.SemaphoreType.DMA((5,)),
            pltpu.VMEM((2,) + shape.shape, BF16),
            pltpu.SemaphoreType.DMA((plan.out_blocks // 2,)),
        ],
        compiler_params=params(),
        name="merge",
    )(where, rng_blocks, ang_blocks, *flat, rng_mats, ang_mats, last_mats)


def focus(plan, where, own, other, owners, groups):
    half = plan.total_rows // 2
    columns = plan.out_blocks * TILE

    def body(
        where_ref, own_ref, oth_ref, owners_ref, image_ref, grad_ref, held_ref, sem
    ):
        side = where_ref[1]
        row = lax.broadcasted_iota(jnp.int32, (STRIP, TILE), 0) + side * half
        mine, theirs = [], []
        stores = []
        for j in range(plan.out_blocks):
            at = j * PAIR
            sums = [jnp.zeros((8, TILE), F32)] * 2
            for top in range(0, half, STRIP):
                strip = slice(top, top + STRIP)
                weight = 1.0 + 2.0 * (row + top).astype(F32) / (plan.total_rows - 1)
                own_re = own_ref[strip, at : at + TILE].astype(F32)
                own_im = own_ref[strip, at + TILE : at + PAIR].astype(F32)
                oth_re = oth_ref[strip, at : at + TILE].astype(F32)
                oth_im = oth_ref[strip, at + TILE : at + PAIR].astype(F32)
                re = own_re + oth_re
                im = own_im + oth_im
                held_ref[0, strip, j * TILE : (j + 1) * TILE] = re.astype(BF16)
                held_ref[1, strip, j * TILE : (j + 1) * TILE] = im.astype(BF16)
                power = weight * (re * re + im * im)
                for which, (a, b) in enumerate(((own_re, own_im), (oth_re, oth_im))):
                    term = power * (re * a + im * b)
                    sums[which] = sums[which] + jnp.sum(
                        term.reshape(STRIP // 8, 8, TILE), axis=0
                    )
            stores.append(
                pltpu.make_async_copy(
                    held_ref.at[:, :, j * TILE : (j + 1) * TILE],
                    image_ref.at[:, :, j * TILE : (j + 1) * TILE],
                    sem.at[j],
                )
            )
            stores[-1].start()
            mine.append(jnp.sum(sums[0], axis=0, keepdims=True))
            theirs.append(jnp.sum(sums[1], axis=0, keepdims=True))
        mine = jnp.concatenate(mine, axis=1) / plan.total_rows
        theirs = jnp.concatenate(theirs, axis=1) / plan.total_rows
        zeroth = jnp.where(side == 0, mine, theirs)
        oneth = jnp.where(side == 0, theirs, mine)
        marks = owners_ref[...] == lax.broadcasted_iota(
            jnp.int32, (groups, columns), 0
        )
        for q, slope in ((0, zeroth), (1, oneth)):
            grad_ref[q] = jnp.sum(jnp.where(marks, slope, 0.0), axis=1, keepdims=True)
        for store in stores:
            store.wait()

    return pl.pallas_call(
        body,
        out_shape=[
            jax.ShapeDtypeStruct((2, half, columns), BF16),
            jax.ShapeDtypeStruct((2, groups, 1), F32),
        ],
        in_specs=[SMEM, VMEM, VMEM, VMEM],
        out_specs=[ANY, VMEM],
        scratch_shapes=[
            pltpu.VMEM((2, half, columns), BF16),
            pltpu.SemaphoreType.DMA((plan.out_blocks,)),
        ],
        compiler_params=params(),
        name="focus",
    )(where, own, other, owners)


def shards(subimages, rng_taps, rng_blocks, rng_weights, ang_taps, ang_blocks, ang_weights, owners):
    panels = lax.axis_size("panel")
    panel = lax.axis_index("panel").astype(jnp.int32)
    side = lax.axis_index("aper").astype(jnp.int32)
    groups = GRP_DEV * panels
    plan = Plan(panels, subimages.shape[2], subimages.shape[3])
    where = jnp.stack([panel, side])

    def plane_shift(step):
        return [
            (g * plan.cells + c, ((g + step) % plan.planes) * plan.cells + c)
            for g in range(plan.planes)
            for c in range(plan.cells)
        ]

    def cell_flip(flip):
        return [(i, i ^ flip) for i in range(panels)]

    steps = [
        sorted({step, plan.planes - step}) for step in range(1, plan.planes // 2 + 1)
    ]
    order = [[0]] + steps
    rest = [step for group in steps[1:] for step in group]
    soon, _ = pack_own(plan, where, subimages, steps[0], [])
    _, near_parts = pack_own(plan, where, subimages, [], range(1, plan.cells))
    later, _ = pack_own(plan, where, subimages, rest, [])
    far = dict(zip(steps[0] + rest, list(soon) + list(later)))

    def across(pieces):
        return [
            lax.ppermute(pieces[flip - 1], "panel", cell_flip(flip))
            for flip in range(1, plan.cells)
        ]

    parts = []
    held = {0: subimages}
    packed = near_parts
    arrived = {
        step: lax.ppermute(far[step], "panel", plane_shift(step))
        for group in steps
        for step in group
    }
    for group in steps:
        received = [arrived[step] for step in group]
        parts.append(across(packed))
        tied = [parts[-1][0]] if len(parts) > 1 else parts[-1]
        tied, received = lax.optimization_barrier((tied, received))
        parts[-1][: len(tied)] = tied
        held.update(zip(group, received))
        packed = pack_panels(plan, where, received)
    parts.append(across(packed))
    held = [held[step] for step in range(plan.planes)]

    first = plan.merged_start(panel)
    near = first + jnp.arange(plan.merged_window, dtype=jnp.int32)
    merge_at = jnp.concatenate([near, 2 * plan.in_blocks + near])
    last_at = (
        4 * plan.in_blocks
        + panel * plan.out_blocks
        + jnp.arange(plan.out_blocks, dtype=jnp.int32)
    )
    ang_mats = build_angle(merge_at, ang_taps, ang_weights[0])
    last_mats = build_angle(last_at, ang_taps, ang_weights[0])
    rng_mats = build_range(plan, rng_taps[0], rng_weights[0])

    own, send = merge(
        plan, where, order, parts, held, rng_blocks[0], ang_blocks, rng_mats, ang_mats, last_mats
    )
    other = lax.ppermute(send, "aper", [(0, 1), (1, 0)])
    columns = plan.out_blocks * TILE
    mine = lax.dynamic_slice_in_dim(owners[None], panel * columns, columns, 1)
    image, partials = focus(plan, where, own, other, mine, groups)
    pieces = lax.all_to_all(
        partials.reshape(2 * panels, GRP_DEV), ("aper", "panel"), 0, 0, tiled=True
    )
    return image, jnp.sum(pieces, axis=0)[None]


def solution(mesh):
    return jax.shard_map(
        shards,
        mesh=mesh,
        in_specs=(
            P(("scene", "aper"), None, "panel", None),
            P("aper", None, None),
            P("aper", None, None),
            P("aper", None, None, None, None),
            P("aper", None),
            P("aper", None),
            P("aper", None, None, None),
            P(),
        ),
        out_specs=(P(None, ("scene", "aper"), "panel"), P(("scene", "aper"), "panel")),
        check_vma=False,
    )
```
